32 devices in a mesh: req: 4 (over z), seq: 8 (over y, x, core).
Axes of the slice: x: 2, y: 2, z: 4, core: 2. Of those that a mesh axis runs over, the one named last changes fastest.
Arguments:
- prompts: bfloat16 [24, 2048, 1024], P('req', 'seq'), may hold values from -6 to 6
- perm: int32 [24], replicated, may hold values from 0 to 23, each once
- lengths: int32 [24], replicated, may hold values from 512 to 2048, as said below
- norm_attn: float32 [1024], replicated, may hold values from 0.25 to 1.75
- norm_mlp: float32 [1024], replicated, may hold values from 0.25 to 1.75
- qkv_train: float32 [1024, 3072], P('seq', 'req'), may hold values from -0.1875 to 0.1875
- qkv_bias: float32 [3072], replicated, may hold values from -3 to 3
- out_train: float32 [1024, 1024], P('seq', 'req'), may hold values from -0.1875 to 0.1875
- gateup_train: float32 [1024, 5632], P('seq', 'req'), may hold values from -0.1875 to 0.1875
- down_train: float32 [2816, 1024], P('seq', 'req'), may hold values from -0.109375 to 0.109375
Outputs:
- states: bfloat16 [24, 2048, 1024], P('req', 'seq')
- key_cache: bfloat16 [24, 2048, 1024], P('req', 'seq')
- value_cache: bfloat16 [24, 2048, 1024], P('req', 'seq')
The draws below stay inside these ranges and needn't reach their ends.
Inputs may be any that keep to these rules, and one draw needn't show every extreme that they name: Valid lengths; some prompt has exactly 2048 and some exactly 512.
All inputs are finite; a program needn't handle non-finite values.
Results may differ from the reference program's by a relative error of at most 0.0085.
Values may be sent and summed in bfloat16 or wider, within the bound.
No kernel may reach another device: no remote copies, remote signals or barrier semaphores. Data moves between devices by JAX's collectives and lax.ppermute only.
A program may use at most 320 MiB of HBM per device.

```python
import jax
import jax.numpy as jnp
from jax import lax

D = 1024
HEADS = 16
HD = 64
FF = 2816
LEN = 2048
PROMPTS = 24


def draw_lengths(key, part):
    first, second = jax.random.split(jax.random.fold_in(key, 17))
    base = jax.random.randint(first, (PROMPTS,), LEN // 4, LEN + 1)
    order = jax.random.permutation(second, PROMPTS)
    base = base.at[order[0]].set(LEN)
    base = base.at[order[1]].set(LEN // 4)
    return base.astype(jnp.int32)


def level_of(rng, extent, pieces, smallest, top_value):
    level, own = 1.0, jax.random.fold_in(rng, 6)
    for dim, blocks in pieces:
        steps = jnp.exp(jax.random.uniform(jax.random.fold_in(own, dim), (blocks,), jnp.float32, smallest / len(pieces), top_value / len(pieces)))
        level = level * jnp.repeat(steps, extent[dim] // blocks).reshape([-1 if axis == dim else 1 for axis in range(len(extent))])
    return level


def scatter_about(rng, dims, deviation, bound, shards=(), kind=jnp.bfloat16):
    factor_of = level_of(rng, dims, shards, -0.22, 0.18) if shards else 1.0
    entries = jax.random.normal(rng, dims, jnp.float32) * deviation * factor_of
    return jnp.minimum(jnp.maximum(entries, -bound), bound).astype(kind)


def setup_inputs(seed: int = 0) -> dict:
    seeds = jax.random.split(jax.random.key(seed), 11)
    return {
        "prompts": scatter_about(seeds[0], (PROMPTS, LEN, D), 1.0, 6.0, ((0, 4), (1, 8))),
        "perm": jax.random.permutation(seeds[1], PROMPTS).astype(jnp.int32),
        "lengths": draw_lengths(jax.random.fold_in(seeds[10], 71), 0),
        "norm_attn": jnp.clip(1.0 + 0.15 * jax.random.normal(seeds[3], (D,), jnp.float32), 0.25, 1.75),
        "norm_mlp": jnp.clip(1.0 + 0.15 * jax.random.normal(seeds[4], (D,), jnp.float32), 0.25, 1.75),
        "qkv_train": scatter_about(seeds[5], (D, 3 * D), D ** -0.5, 0.1875, ((0, 8), (1, 4)), jnp.float32),
        "qkv_bias": scatter_about(seeds[6], (3 * D,), 0.5, 3.0, (), jnp.float32),
        "out_train": scatter_about(seeds[7], (D, D), D ** -0.5, 0.1875, ((0, 8), (1, 4)), jnp.float32),
        "gateup_train": scatter_about(seeds[8], (D, 2 * FF), D ** -0.5, 0.1875, ((0, 8), (1, 4)), jnp.float32),
        "down_train": scatter_about(seeds[9], (FF, D), FF ** -0.5, 0.109375, ((0, 8), (1, 4)), jnp.float32),
    }


def rms_scale(rows, gain):
    rows = rows.astype(jnp.float32)
    return rows * lax.rsqrt(lax.optimization_barrier(jnp.mean(rows * rows, axis=-1, keepdims=True)) + 1e-06) * gain

def rotate(block, positions):
    half = HD // 2
    count = block.shape[0]
    freqs = jnp.power(1000000.0, -2.0 * jnp.arange(half).astype(jnp.float32) / HD)
    angle = positions[:, None] * freqs[None, :]
    cosine = jnp.cos(angle)[:, None, :]
    sine = jnp.sin(angle)[:, None, :]
    heads = block.reshape(count, -1, HD)
    first = heads[:, :, :half]
    second = heads[:, :, half:]
    turned = jnp.concatenate([first * cosine - second * sine, second * cosine + first * sine], axis=-1)
    return turned.reshape(count, -1)

def attend_one(items):
    query, keys, values = items
    query = query.reshape(LEN, HEADS, HD).astype(jnp.float32)
    keys = keys.reshape(LEN, HEADS, HD).astype(jnp.float32)
    values = values.reshape(LEN, HEADS, HD).astype(jnp.float32)
    scores = jnp.einsum('ihd,jhd->hij', query, keys) * HD ** (-0.5)
    causal = jnp.arange(LEN)[None, :] <= jnp.arange(LEN)[:, None]
    scores = jnp.where(causal[None], scores, -1e+30)
    top = lax.optimization_barrier(jnp.max(scores, axis=-1, keepdims=True))
    expo = jnp.exp(scores - top)
    probs = (expo / lax.optimization_barrier(jnp.sum(expo, axis=-1, keepdims=True))).astype(jnp.bfloat16)
    out = jnp.einsum('hij,jhd->ihd', probs.astype(jnp.float32), values)
    return out.astype(jnp.bfloat16).reshape(LEN, D)

def reference(prompts, perm, lengths, norm_attn, norm_mlp, qkv_train, qkv_bias, out_train, gateup_train, down_train):
    dealt = prompts[perm]
    slot_len = lengths[perm]
    valid = (jnp.arange(LEN, dtype=jnp.int32)[None, :] < slot_len[:, None]).astype(jnp.float32)
    rows = dealt.reshape(PROMPTS * LEN, D)
    positions = jnp.tile(jnp.arange(LEN, dtype=jnp.int32), PROMPTS).astype(jnp.float32)
    normed = rms_scale(rows, norm_attn).astype(jnp.bfloat16)
    qkv = jnp.dot(normed, qkv_train.astype(jnp.bfloat16), preferred_element_type=jnp.float32) + qkv_bias
    query = rotate(qkv[:, :D], positions).astype(jnp.bfloat16).reshape(PROMPTS, LEN, D)
    keys = rotate(qkv[:, D:2 * D], positions).astype(jnp.bfloat16).reshape(PROMPTS, LEN, D)
    values = qkv[:, 2 * D:].astype(jnp.bfloat16).reshape(PROMPTS, LEN, D)
    keep = valid.astype(jnp.bfloat16)[:, :, None]
    key_cache = keys * keep
    value_cache = values * keep
    attended = lax.map(attend_one, (query, keys, values)).reshape(PROMPTS * LEN, D)
    mid = rows.astype(jnp.float32) + jnp.dot(attended, out_train.astype(jnp.bfloat16), preferred_element_type=jnp.float32)
    normed2 = rms_scale(mid, norm_mlp).astype(jnp.bfloat16)
    both = jnp.dot(normed2, gateup_train.astype(jnp.bfloat16), preferred_element_type=jnp.float32)
    hidden = (jax.nn.silu(both[:, :FF]) * both[:, FF:]).astype(jnp.bfloat16)
    final = mid + jnp.dot(hidden, down_train.astype(jnp.bfloat16), preferred_element_type=jnp.float32)
    final = (final * valid.reshape(PROMPTS * LEN, 1)).astype(jnp.bfloat16).reshape(PROMPTS, LEN, D)
    inverse = jnp.argsort(perm).astype(jnp.int32)
    states = final[inverse]
    return (states, key_cache, value_cache)
```

```python
import functools

import jax
import jax.numpy as jnp
from jax import lax
from jax.experimental import pallas as pl
from jax.experimental.pallas import tpu as pltpu
from jax.sharding import PartitionSpec as P

HEADS = 16
HD = 64
BF = jnp.bfloat16
F32 = jnp.float32
LOG2E = 1.4426950408889634
VMEM = 56 * 1024 * 1024


def rms_scale(rows, gain):
    rows = rows.astype(F32)
    return rows * lax.rsqrt(jnp.mean(rows * rows, axis=-1, keepdims=True) + 1e-06) * gain


def swap(array, mask):
    groups = lax.axis_size("seq")
    return lax.ppermute(array, "seq", [(i, i ^ mask) for i in range(groups)])


def spread(array, first, second):
    if lax.axis_size("seq") != 8:
        return [lax.all_gather(array, "seq", axis=1, tiled=True)[None]]
    held = {0: array}
    for mask in (first, second, 1):
        for m in sorted(held):
            held[m ^ mask] = swap(held[m], mask)
    return [held[m] for m in range(8)]


def sources(refs, me):
    if len(refs) == 1:
        return [(refs[0].at[g], g) for g in range(refs[0].shape[0])]
    return [(ref, jnp.bitwise_xor(me, m)) for m, ref in enumerate(refs)]


def tables(length):
    half = HD // 2
    freqs = jnp.power(1000000.0, -2.0 * jnp.arange(half).astype(F32) / HD)
    angle = jnp.arange(length, dtype=jnp.int32).astype(F32)[:, None] * freqs[None, :]
    cosine = jnp.cos(angle)
    sine = jnp.sin(angle)
    return (
        jnp.concatenate([cosine] * (128 // half), axis=1),
        jnp.concatenate([-sine, sine] * (64 // half), axis=1),
    )


def turn(block, cosine, sine):
    rows, width = block.shape
    half = HD // 2
    if width < 128:
        cosine, sine = cosine[:, :width], sine[:, :width]
    elif width > 128:
        cosine = jnp.concatenate([cosine] * (width // 128), axis=1)
        sine = jnp.concatenate([sine] * (width // 128), axis=1)
    if width < 128:
        other = jnp.concatenate([block[:, half:], block[:, :half]], axis=1)
    else:
        lane = lax.broadcasted_iota(jnp.int32, block.shape, 1)
        low = (lane % HD) < half
        other = jnp.where(low, pltpu.roll(block, width - half, 1), pltpu.roll(block, half, 1))
    return block * cosine + other * sine


def attend_kernel(count, tok, heads, chunk, blocks, info, lens, *refs):
    x_refs, refs = refs[:count], refs[count:]
    w_refs, refs = refs[:count], refs[count:]
    bias, cos_ref, sin_ref, out_ref, xs, ws, qs, ks, vs, sems = refs
    me = info[1]
    slot = info[2]
    length = lens[slot]
    total = xs.shape[0]
    groups = total // tok
    blk = min(256, total)
    width = heads * HD
    rows_w = w_refs[0].shape[-2]
    which = lax.rem(me, groups // 2)
    copies = []

    def copy_of(source, target):
        copies.append(pltpu.make_async_copy(source, target, sems.at[len(copies)]))

    for ref, at in sources(x_refs, me):
        copy_of(ref, xs.at[pl.ds(pl.multiple_of(at * tok, tok), tok), :])
    for ref, at in sources(w_refs, me):
        place = pl.ds(pl.multiple_of(at * rows_w, rows_w), rows_w)
        if chunk == width:
            for part in range(3):
                n = part * (HEADS // heads) + which
                k = lax.div(n, blocks)
                off = pl.multiple_of(lax.rem(n, blocks) * chunk, chunk)
                copy_of(
                    ref.at[k, :, pl.ds(off, chunk)], ws.at[place, pl.ds(part * width, width)]
                )
        else:
            copy_of(ref, ws.at[place, :])
    for copy in copies:
        copy.start()
    ones = jnp.where(
        lax.broadcasted_iota(jnp.int32, (blk, 128 - HD), 1) == 0, 1.0, 0.0
    ).astype(BF)
    for copy in copies:
        copy.wait()
    steps = lax.div(length + (blk - 1), blk)

    def project(i, carry):
        place = pl.ds(pl.multiple_of(i * blk, blk), blk)
        qkv = jnp.dot(xs[place, :], ws[...], preferred_element_type=F32) + bias[...]
        cosine, sine = cos_ref[place, :], sin_ref[place, :]
        query = turn(qkv[:, :width], cosine, sine).astype(BF)
        keys = turn(qkv[:, width : 2 * width], cosine, sine).astype(BF)
        values = qkv[:, 2 * width :].astype(BF)
        for h in range(heads):
            cols = slice(h * HD, (h + 1) * HD)
            qs[h, place, :] = query[:, cols]
            ks[h, place, :] = keys[:, cols]
            vs[h, place, :] = jnp.concatenate([values[:, cols], ones], axis=1)
        return carry

    lax.fori_loop(0, steps, project, 0)
    causal = lax.broadcasted_iota(jnp.int32, (blk, blk), 1) <= lax.broadcasted_iota(
        jnp.int32, (blk, blk), 0
    )
    factor = HD ** (-0.5) * LOG2E
    for i in range(total // blk):
        span = (i + 1) * blk
        place = slice(i * blk, span)

        @pl.when(i * blk < length)
        def _():
            for h in range(heads):
                scores = lax.dot_general(
                    qs[h, place, :],
                    ks[h, :span, :],
                    (((1,), (1,)), ((), ())),
                    preferred_element_type=F32,
                )
                last = jnp.where(causal, scores[:, i * blk :], -1e30)
                if i:
                    scores = jnp.concatenate([scores[:, : i * blk], last], axis=1)
                else:
                    scores = last
                top = jnp.max(scores, axis=-1, keepdims=True)
                expo = jnp.exp2((scores - top) * factor).astype(BF)
                mixed = jnp.dot(expo, vs[h, :span, :], preferred_element_type=F32)
                out_ref[place, h * HD : (h + 1) * HD] = (
                    mixed[:, :HD] / mixed[:, HD : HD + 1]
                ).astype(BF)

        @pl.when(i * blk >= length)
        def _():
            out_ref[place, :] = jnp.zeros((blk, width), BF)


def mlp_kernel(count, tok, info, lens, *refs):
    x_ref, refs = refs[0], refs[1:]
    a_refs, refs = refs[:3], refs[3:]
    out_refs, refs = refs[:count], refs[count:]
    gu_refs, refs = refs[:count], refs[count:]
    down_refs, refs = refs[:count], refs[count:]
    gain, states, att, wo, wg, wd, sems = refs
    req, me = info[0], info[1]
    step = pl.program_id(0)
    thirds = pl.num_programs(0) // 2
    j = lax.div(step, 2)
    half = lax.rem(step, 2)
    groups = att.shape[1]
    blocks = wo.shape[0]

    def loads(refs, dest, first):
        rows = refs[0].shape[-2]
        return [
            pltpu.make_async_copy(
                ref, dest.at[:, pl.ds(pl.multiple_of(at * rows, rows), rows), :], sems.at[first + i]
            )
            for i, (ref, at) in enumerate(sources(refs, me))
        ]

    def load(index):
        if index == 0:
            first = [pltpu.make_async_copy(a_refs[i], att.at[i], sems.at[i]) for i in range(3)]
            return first + loads(out_refs, wo, 3)
        if index == 1:
            return loads(gu_refs, wg, 3 + count)
        return loads(down_refs, wd, 3 + 2 * count)

    def arrive(index):
        @pl.when(step == 0)
        def _():
            for copy in load(index):
                copy.wait()

    @pl.when(step == 0)
    def _():
        for index in range(3):
            for copy in load(index):
                copy.start()

    arrive(0)
    share = groups // 2
    attended = jnp.concatenate([att[j, half * share + h] for h in range(share)], axis=1)
    rows = x_ref[0].astype(F32)
    mid = rows + jnp.concatenate(
        [jnp.dot(attended, wo[k], preferred_element_type=F32) for k in range(blocks)], axis=1
    )
    normed = rms_scale(mid, gain[...]).astype(BF)
    arrive(1)
    hidden = []
    for k in range(blocks // 2):
        gate = jnp.dot(normed, wg[k], preferred_element_type=F32)
        up = jnp.dot(normed, wg[k + blocks // 2], preferred_element_type=F32)
        hidden.append((gate * jax.nn.sigmoid(gate) * up).astype(BF))
    hidden = jnp.concatenate(hidden, axis=1)
    arrive(2)
    final = mid + jnp.concatenate(
        [jnp.dot(hidden, wd[k], preferred_element_type=F32) for k in range(blocks)], axis=1
    )
    places = me * tok + lax.broadcasted_iota(jnp.int32, (tok, 1), 0)
    length = lens[req * (2 * thirds) + half * thirds + j]
    states[0] = jnp.where(places < length, final, 0.0).astype(BF)


def cache_kernel(count, tok, chunk, blocks, info, perm, lens, x_ref, *refs):
    w_refs, refs = refs[:count], refs[count:]
    bias, cos_ref, sin_ref, key_ref, value_ref, ws, sems = refs
    req, me = info[0], info[1]
    step = pl.program_id(0)
    size = pl.num_programs(0)
    rows = w_refs[0].shape[-2]

    @pl.when(step == 0)
    def _():
        pairs = sources(w_refs, me)
        copies = [
            pltpu.make_async_copy(
                ref, ws.at[:, pl.ds(pl.multiple_of(at * rows, rows), rows), :], sems.at[i]
            )
            for i, (ref, at) in enumerate(pairs)
        ]
        for copy in copies:
            copy.start()
        for copy in copies:
            copy.wait()

    normed = x_ref[0]
    places = me * tok + lax.broadcasted_iota(jnp.int32, (tok, 1), 0)
    valid = places < lens[perm[req * size + step]]
    model = key_ref.shape[-1]
    per = model // chunk
    for n in range(per, 3 * per):
        weights = ws[n // blocks, :, (n % blocks) * chunk : (n % blocks + 1) * chunk]
        piece = jnp.dot(normed, weights, preferred_element_type=F32)
        piece = piece + bias[:, n * chunk : (n + 1) * chunk]
        cols = slice((n % per) * chunk, (n % per + 1) * chunk)
        if n < 2 * per:
            piece = turn(piece, cos_ref[...], sin_ref[...])
            key_ref[0, :, cols] = jnp.where(valid, piece, 0.0).astype(BF)
        else:
            value_ref[0, :, cols] = jnp.where(valid, piece, 0.0).astype(BF)


def local(
    prompts,
    perm,
    lengths,
    norm_attn,
    norm_mlp,
    qkv_train,
    qkv_bias,
    out_train,
    gateup_train,
    down_train,
):
    count, tok, width = prompts.shape
    groups = lax.axis_size("seq")
    parts = lax.axis_size("req")
    total = groups * tok
    me = lax.axis_index("seq").astype(jnp.int32)
    req = lax.axis_index("req").astype(jnp.int32)
    share = groups // 2
    heads = HEADS // share
    thirds = count // 2
    half = lax.div(me, jnp.int32(share))
    which = lax.rem(me, jnp.int32(share))
    own_w = heads * HD
    chunk = 256
    blocks = qkv_train.shape[1] // chunk
    anywhere = pl.BlockSpec(memory_space=pl.ANY)

    normed = rms_scale(prompts, norm_attn).astype(BF)

    def columns(trained):
        return lax.all_gather(trained.astype(BF), "req", axis=0)

    qkv_w = spread(columns(qkv_train), 4, 2)
    out_w = spread(columns(out_train), 2, 4)
    gu_w = spread(columns(gateup_train), 2, 4)
    down_w = spread(columns(down_train), 2, 4)

    cosine, sine = tables(total)

    if groups == 8:
        x_parts = []
        for j in range(thirds):
            mine = lax.dynamic_index_in_dim(normed, half * thirds + j, 0, keepdims=False)
            other = lax.dynamic_index_in_dim(normed, (1 - half) * thirds + j, 0, keepdims=False)
            held = {0: mine, 4: swap(other, 4)}
            for mask in (2, 1):
                for m in sorted(held):
                    held[m ^ mask] = swap(held[m], mask)
            x_parts.append([held[m] for m in range(8)])
    else:
        everything = lax.all_gather(normed, "seq", axis=0)
        x_parts = [
            [lax.dynamic_index_in_dim(everything, half * thirds + j, 1, keepdims=False)]
            for j in range(thirds)
        ]

    bias = lax.dynamic_index_in_dim(
        qkv_bias.reshape(3, share, own_w), which, 1, keepdims=False
    ).reshape(1, 3 * own_w)
    if own_w == chunk:
        attend_w = qkv_w
    else:
        full = qkv_w[0][0].transpose(1, 0, 2).reshape(width, 3, share, own_w)
        mine = lax.dynamic_index_in_dim(full, which, 2, keepdims=False)
        attend_w = [mine.reshape(1, width, 3 * own_w)]

    n_x, n_w = len(x_parts[0]), len(attend_w)
    attended = []
    for j in range(thirds):
        info = jnp.stack([req, me, req * count + half * thirds + j, jnp.int32(groups)])
        out = pl.pallas_call(
            functools.partial(attend_kernel, n_x, tok, heads, chunk, blocks),
            out_shape=jax.ShapeDtypeStruct((total, own_w), BF),
            grid_spec=pltpu.PrefetchScalarGridSpec(
                num_scalar_prefetch=2,
                grid=(1,),
                in_specs=[anywhere] * (n_x + n_w)
                + [
                    pl.BlockSpec((1, 3 * own_w), lambda i, *_: (0, 0)),
                    pl.BlockSpec((total, 128), lambda i, *_: (0, 0)),
                    pl.BlockSpec((total, 128), lambda i, *_: (0, 0)),
                ],
                out_specs=pl.BlockSpec((total, own_w), lambda i, *_: (0, 0)),
                scratch_shapes=[
                    pltpu.VMEM((total, width), BF),
                    pltpu.VMEM((width, 3 * own_w), BF),
                    pltpu.VMEM((heads, total, HD), BF),
                    pltpu.VMEM((heads, total, HD), BF),
                    pltpu.VMEM((heads, total, 128), BF),
                    pltpu.SemaphoreType.DMA((groups + 3 * n_w,)),
                ],
            ),
            compiler_params=pltpu.CompilerParams(vmem_limit_bytes=VMEM),
            cost_estimate=pl.CostEstimate(
                flops=25_000_000_000, bytes_accessed=8_000_000, transcendentals=0
            ),
            name="attend",
        )(info, lengths, *x_parts[j], *attend_w, bias, cosine, sine)
        attended.append(
            lax.all_to_all(
                out.reshape(groups, tok, own_w), "seq", split_axis=0, concat_axis=0, tiled=True
            )
        )

    info = jnp.stack([req, me, jnp.int32(0), jnp.int32(groups)])
    n_w = len(out_w)

    def prompt_at(i, *_):
        return (lax.rem(i, 2) * thirds + lax.div(i, 2), 0, 0)

    states = pl.pallas_call(
        functools.partial(mlp_kernel, n_w, tok),
        out_shape=jax.ShapeDtypeStruct((count, tok, width), BF),
        grid_spec=pltpu.PrefetchScalarGridSpec(
            num_scalar_prefetch=2,
            grid=(count,),
            in_specs=[pl.BlockSpec((1, tok, width), prompt_at)]
            + [anywhere] * (thirds + 3 * n_w)
            + [pl.BlockSpec((1, width), lambda i, *_: (0, 0))],
            out_specs=pl.BlockSpec((1, tok, width), prompt_at),
            scratch_shapes=[
                pltpu.VMEM((thirds, groups, tok, own_w), BF),
                pltpu.VMEM((parts, width, out_train.shape[1]), BF),
                pltpu.VMEM((parts, width, gateup_train.shape[1]), BF),
                pltpu.VMEM((parts, groups * down_train.shape[0], down_train.shape[1]), BF),
                pltpu.SemaphoreType.DMA((thirds + 3 * n_w,)),
            ],
        ),
        compiler_params=pltpu.CompilerParams(vmem_limit_bytes=VMEM),
        cost_estimate=pl.CostEstimate(
            flops=30_000_000_000, bytes_accessed=26_000_000, transcendentals=0
        ),
        name="feed_forward",
    )(info, lengths, prompts, *attended, *out_w, *gu_w, *down_w, norm_mlp.reshape(1, width))

    everyone = lax.all_gather(normed, "req", axis=0, tiled=True)
    own_rows = pl.BlockSpec((tok, 128), lambda i, info, *_: (info[1], 0))
    n_w = len(qkv_w)
    keys, values = pl.pallas_call(
        functools.partial(cache_kernel, n_w, tok, chunk, blocks),
        out_shape=[jax.ShapeDtypeStruct((count, tok, width), BF)] * 2,
        grid_spec=pltpu.PrefetchScalarGridSpec(
            num_scalar_prefetch=3,
            grid=(count,),
            in_specs=[
                pl.BlockSpec(
                    (1, tok, width), lambda i, info, perm, lens: (perm[info[0] * count + i], 0, 0)
                )
            ]
            + [anywhere] * n_w
            + [
                pl.BlockSpec((1, 3 * width), lambda i, *_: (0, 0)),
                own_rows,
                own_rows,
            ],
            out_specs=[pl.BlockSpec((1, tok, width), lambda i, *_: (i, 0, 0))] * 2,
            scratch_shapes=[
                pltpu.VMEM((parts, width, qkv_train.shape[1]), BF),
                pltpu.SemaphoreType.DMA((n_w,)),
            ],
        ),
        compiler_params=pltpu.CompilerParams(vmem_limit_bytes=VMEM),
        cost_estimate=pl.CostEstimate(
            flops=8_000_000_000, bytes_accessed=16_000_000, transcendentals=0
        ),
        name="caches",
    )(info, perm, lengths, everyone, *qkv_w, qkv_bias.reshape(1, 3 * width), cosine, sine)
    return (states, keys, values)


def solution(mesh):
    placed = (
        P("req", "seq", None),
        P(),
        P(),
        P(),
        P(),
        P("seq", "req"),
        P(),
        P("seq", "req"),
        P("seq", "req"),
        P("seq", "req"),
    )
    return jax.shard_map(
        local,
        mesh=mesh,
        in_specs=placed,
        out_specs=(P("req", "seq", None), P("req", "seq", None), P("req", "seq", None)),
        check_vma=False,
    )
```

```python
import functools

import jax
import jax.numpy as jnp
import numpy as np
from jax import lax
from jax.experimental import pallas as pl
from jax.experimental.pallas import tpu as pltpu
from jax.sharding import PartitionSpec as P

HEADS = 16
HD = 64
BF = jnp.bfloat16
F32 = jnp.float32
LOG2E = 1.4426950408889634
VMEM = 56 * 1024 * 1024
MASKS = (0, 2, 4, 6)
PAIRS = (((0, 2), 0), ((0, 4), 1), ((4, 6), 0), ((2, 6), 1))


def rms_scale(rows, gain):
    rows = rows.astype(F32)
    return rows * lax.rsqrt(jnp.mean(rows * rows, axis=-1, keepdims=True) + 1e-06) * gain


def swap(array, mask):
    groups = lax.axis_size("seq")
    return lax.ppermute(array, "seq", [(i, i ^ mask) for i in range(groups)])


def after(array, *others):
    return lax.optimization_barrier((array, *others))[0]


def whole(array):
    return [lax.all_gather(array, "seq", axis=1, tiled=True)[None]]


def ring_order():
    parts = lax.axis_size("req")
    return list(range(1, parts, 2)) + list(range(0, parts, 2))[::-1]


def hop(array):
    order = ring_order()
    return lax.ppermute(
        array, "req", [(order[i], order[(i + 1) % len(order)]) for i in range(len(order))]
    )


def steps_back():
    order = ring_order()
    place = np.argsort(np.array(order)).astype(np.int32)
    here = jnp.take(jnp.asarray(place), lax.axis_index("req"))
    return lax.rem(here - place + np.int32(len(order)), jnp.int32(len(order)))


def gate(held):
    return lax.optimization_barrier(tuple(held))


def sources(refs, me):
    rows = refs[0].shape[-2]
    if len(refs) == 1:
        return [(refs[0].at[g], g * rows, g) for g in range(refs[0].shape[0])]
    found = []
    half = len(refs) // 2
    for n, ref in enumerate(refs):
        core = n // half
        masks, part = (MASKS, 0) if half == 1 else PAIRS[n % half]
        parts = 1 if half == 1 else 2
        for i, mask in enumerate(masks):
            whose = jnp.bitwise_xor(me, mask ^ core)
            found.append((ref.at[i], pl.multiple_of((whose * parts + part) * rows, rows), part))
    return found


def tables(length):
    half = HD // 2
    freqs = np.power(1000000.0, -2.0 * np.arange(half) / HD)
    angle = np.arange(length)[:, None] * freqs[None, :]
    cosine = np.cos(angle).astype(np.float32)
    sine = np.sin(angle).astype(np.float32)
    return (
        jnp.asarray(np.concatenate([cosine] * (128 // half), axis=1)),
        jnp.asarray(np.concatenate([-sine, sine] * (64 // half), axis=1)),
    )


def turn(block, cosine, sine):
    rows, width = block.shape
    half = HD // 2
    if width < 128:
        cosine, sine = cosine[:, :width], sine[:, :width]
    elif width > 128:
        cosine = jnp.concatenate([cosine] * (width // 128), axis=1)
        sine = jnp.concatenate([sine] * (width // 128), axis=1)
    if width < 128:
        other = jnp.concatenate([block[:, half:], block[:, :half]], axis=1)
    else:
        lane = lax.broadcasted_iota(jnp.int32, block.shape, 1)
        low = (lane % HD) < half
        other = jnp.where(low, pltpu.roll(block, width - half, 1), pltpu.roll(block, half, 1))
    return block * cosine + other * sine


def attend_kernel(j, count, count_w, tok, heads, chunk, blocks, info, lens, *refs):
    x_refs, refs = refs[:count], refs[count:]
    w_refs, refs = refs[:count_w], refs[count_w:]
    if count > 1:
        x_refs = [ref.at[j] for ref in x_refs]
    bias, cos_ref, sin_ref, out_ref, xs, ws, qs, ks, vs, sems = refs
    me = info[1]
    slot = info[2]
    length = lens[slot]
    total = xs.shape[0]
    groups = total // tok
    blk = min(256, total)
    width = heads * HD
    rows_w = w_refs[0].shape[-2]
    which = info[3]
    copies = []

    def copy_of(source, target):
        copies.append(pltpu.make_async_copy(source, target, sems.at[len(copies)]))

    for ref, at, _ in sources(x_refs, me):
        copy_of(ref, xs.at[pl.ds(at, tok), :])
    for ref, at, _ in sources(w_refs, me):
        place = pl.ds(at, rows_w)
        if chunk == width:
            for part in range(3):
                n = part * (HEADS // heads) + which
                k = info[4 + lax.div(n, blocks)]
                off = pl.multiple_of(lax.rem(n, blocks) * chunk, chunk)
                copy_of(
                    ref.at[k, :, pl.ds(off, chunk)], ws.at[place, pl.ds(part * width, width)]
                )
        else:
            copy_of(ref, ws.at[place, :])
    for copy in copies:
        copy.start()
    ones = jnp.where(
        lax.broadcasted_iota(jnp.int32, (blk, 128 - HD), 1) == 0, 1.0, 0.0
    ).astype(BF)
    for copy in copies:
        copy.wait()
    steps = lax.div(length + (blk - 1), blk)

    def project(i, carry):
        place = pl.ds(pl.multiple_of(i * blk, blk), blk)
        qkv = jnp.dot(xs[place, :], ws[...], preferred_element_type=F32) + bias[...]
        cosine, sine = cos_ref[place, :], sin_ref[place, :]
        query = turn(qkv[:, :width], cosine, sine).astype(BF)
        keys = turn(qkv[:, width : 2 * width], cosine, sine).astype(BF)
        values = qkv[:, 2 * width :].astype(BF)
        for h in range(heads):
            cols = slice(h * HD, (h + 1) * HD)
            qs[h, place, :] = query[:, cols]
            ks[h, place, :] = keys[:, cols]
            vs[h, place, :] = jnp.concatenate([values[:, cols], ones], axis=1)
        return carry

    lax.fori_loop(0, steps, project, 0)
    causal = lax.broadcasted_iota(jnp.int32, (blk, blk), 1) <= lax.broadcasted_iota(
        jnp.int32, (blk, blk), 0
    )
    factor = HD ** (-0.5) * LOG2E
    for i in range(total // blk):
        span = (i + 1) * blk
        place = slice(i * blk, span)

        @pl.when(i * blk < length)
        def _():
            for h in range(heads):
                scores = lax.dot_general(
                    qs[h, place, :],
                    ks[h, :span, :],
                    (((1,), (1,)), ((), ())),
                    preferred_element_type=F32,
                )
                last = jnp.where(causal, scores[:, i * blk :], -1e30)
                if i:
                    scores = jnp.concatenate([scores[:, : i * blk], last], axis=1)
                else:
                    scores = last
                top = jnp.max(scores, axis=-1, keepdims=True)
                expo = jnp.exp2((scores - top) * factor).astype(BF)
                mixed = jnp.dot(expo, vs[h, :span, :], preferred_element_type=F32)
                out_ref[place, h * HD : (h + 1) * HD] = (
                    mixed[:, :HD] / mixed[:, HD : HD + 1]
                ).astype(BF)

        @pl.when(i * blk >= length)
        def _():
            out_ref[place, :] = jnp.zeros((blk, width), BF)


def mlp_kernel(count, tok, bits, chunks, info, lens, *refs):
    x_ref, refs = refs[0], refs[1:]
    thirds = pl.num_programs(0) // 2
    a_refs, refs = refs[: len(chunks)], refs[len(chunks) :]
    gu_refs, refs = refs[:count], refs[count:]
    if count == 1:
        out_refs, down_refs, refs = refs[:1], refs[1:2], refs[2:]
    else:
        tail_refs, refs = refs[:count], refs[count:]
    gain, states, att, wo, wg, wd, sems = refs
    req, me = info[0], info[1]
    step = pl.program_id(0)
    j = lax.div(step, 2)
    half = lax.rem(step, 2)
    groups = att.shape[1]
    blocks = wo.shape[0]

    def pick(items, dest, first):
        return [
            pltpu.make_async_copy(
                ref.at[info[4 + k], pl.ds(start, rows), :],
                dest.at[k, pl.ds(at, rows), :],
                sems.at[first + i * blocks + k],
            )
            for i, (ref, start, at, rows) in enumerate(items)
            for k in range(blocks)
        ]

    def pieces(refs):
        rows = refs[0].shape[-2]
        return [(ref, 0, at, rows) for ref, at, _ in sources(refs, me)]

    def tail_pieces(down):
        rows_o, rows_d = wo.shape[1] // groups, wd.shape[1] // groups
        rows = tail_refs[0].shape[-2]
        items = []
        for ref, at, part in sources(tail_refs, me):
            low, high = part * rows, (part + 1) * rows
            start = max(low, rows_o) if down else low
            stop = high if down else min(high, rows_o)
            if start < stop:
                skip, size = (rows_o, rows_d) if down else (0, rows_o)
                whose = lax.div(at, 2 * rows)
                at = pl.multiple_of(whose * size + (start - skip), 16)
                items.append((ref, start - low, at, stop - start))
        return items

    def load(index):
        first = thirds + index * 2 * groups * blocks
        if index == 1:
            return pick(pieces(gu_refs), wg, first)
        dest = wd if index else wo
        if count == 1:
            items = pieces(down_refs if index else out_refs)
        else:
            items = tail_pieces(index == 2)
        copies = pick(items, dest, first)
        if index == 0:
            copies += [
                pltpu.make_async_copy(
                    ref, att.at[pl.ds(sum(chunks[:i]), chunks[i])], sems.at[i]
                )
                for i, ref in enumerate(a_refs)
            ]
        return copies

    def arrive(index):
        @pl.when(step == 0)
        def _():
            for copy in load(index):
                copy.wait()

    @pl.when(step == 0)
    def _():
        for index in range(3):
            for copy in load(index):
                copy.start()

    arrive(0)
    share = groups // 2
    bit = jnp.where(j == 1, bits[1], bits[0])
    attended = jnp.concatenate(
        [att[j, (lax.div(h, bit) * 2 + half) * bit + lax.rem(h, bit)] for h in range(share)], axis=1
    )
    rows = x_ref[0].astype(F32)
    mid = rows + jnp.concatenate(
        [jnp.dot(attended, wo[k], preferred_element_type=F32) for k in range(blocks)], axis=1
    )
    normed = rms_scale(mid, gain[...]).astype(BF)
    arrive(1)
    hidden = []
    for k in range(blocks // 2):
        gate = jnp.dot(normed, wg[k], preferred_element_type=F32)
        up = jnp.dot(normed, wg[k + blocks // 2], preferred_element_type=F32)
        hidden.append((gate * jax.nn.sigmoid(gate) * up).astype(BF))
    hidden = jnp.concatenate(hidden, axis=1)
    arrive(2)
    final = mid + jnp.concatenate(
        [jnp.dot(hidden, wd[k], preferred_element_type=F32) for k in range(blocks)], axis=1
    )
    places = me * tok + lax.broadcasted_iota(jnp.int32, (tok, 1), 0)
    length = lens[req * (2 * thirds) + half * thirds + j]
    states[0] = jnp.where(places < length, final, 0.0).astype(BF)


def ahead(group, req):
    parts = lax.axis_size("req")
    return lax.rem(group - req + parts, parts)


def route_kernel(per, share, info, perm, normed, packed, color, rank, back, sems):
    count = perm.shape[0]
    req = info[0]

    def place(i, carry):
        back[perm[i]] = i
        color[i] = -1
        return carry

    lax.fori_loop(0, count, place, 0)

    def walk(i, start):
        start = lax.while_loop(lambda p: color[p] >= 0, lambda p: lax.rem(p + 1, count), start)
        mate = jnp.bitwise_xor(start, 1)
        color[start] = 0
        color[mate] = 1
        return perm[jnp.bitwise_xor(back[mate], 1)]

    lax.fori_loop(0, count // 2, walk, jnp.int32(0))

    def number(i, carry):
        first, second, first_slot, second_slot = carry
        fresh = lax.rem(i, per) == 0
        first, second, first_slot, second_slot = (
            jnp.where(fresh, 0, v) for v in (first, second, first_slot, second_slot)
        )
        mine = color[i]
        rank[i] = jnp.where(mine == 0, first, second)
        there = color[perm[i]]
        rank[count + i] = jnp.where(there == 0, first_slot, second_slot)
        return (first + 1 - mine, second + mine, first_slot + 1 - there, second_slot + there)

    lax.fori_loop(0, count, number, (jnp.int32(0),) * 4)
    for p in range(per):
        at = req * per + p
        for part in range(2):
            pltpu.make_async_copy(
                normed.at[p, part],
                packed.at[2 * part + color[at], rank[at]],
                sems.at[p * 2 + part],
            ).start()
    for p in range(per):
        at = req * per + p
        for part in range(2):
            pltpu.make_async_copy(
                normed.at[p, part],
                packed.at[2 * part + color[at], rank[at]],
                sems.at[p * 2 + part],
            ).wait()


def pass_kernel(per, parts, info, perm, color, rank, got, *refs):
    packed, sems = refs[:parts], refs[parts]
    count = perm.shape[0]
    req = info[0]
    shade = lax.rem(req, 2)

    def each(act):
        def slot(i, carry):
            prompt = perm[i]
            far = ahead(lax.div(i, per), req)
            for d in range(parts):

                @pl.when(jnp.logical_and(color[prompt] == shade, far == d))
                def _():
                    act(
                        pltpu.make_async_copy(
                            got.at[lax.div(prompt, per), rank[prompt]],
                            packed[d].at[rank[count + i]],
                            sems.at[i],
                        )
                    )

            return carry

        lax.fori_loop(0, count, slot, 0)

    each(lambda copy: copy.start())
    each(lambda copy: copy.wait())


def cache_kernel(count, tok, chunk, blocks, info, perm, lens, color, rank, *refs):
    w_refs, refs = refs[:count], refs[count:]
    bias, cos_ref, sin_ref, *refs = refs
    got, (key_ref, value_ref, ws, held, sems) = refs[:-5], refs[-5:]
    req, me = info[0], info[1]
    step = pl.program_id(0)
    size = pl.num_programs(0)
    rows = w_refs[0].shape[-2]

    @pl.when(step == 0)
    def _():
        copies = [
            pltpu.make_async_copy(
                ref.at[info[4 + k]], ws.at[k, pl.ds(at, rows), :], sems.at[i * ws.shape[0] + k]
            )
            for i, (ref, at, _) in enumerate(sources(w_refs, me))
            for k in range(ws.shape[0])
        ]
        copies += [
            pltpu.make_async_copy(got[d], held.at[d], sems.at[len(copies) + d])
            for d in range(len(got))
        ]
        for copy in copies:
            copy.start()
        for copy in copies:
            copy.wait()

    prompt = perm[req * size + step]
    at = rank[perm.shape[0] + req * size + step]
    normed = jnp.concatenate(
        [held[ahead(req, 2 * part + color[prompt]), at] for part in range(2)], axis=0
    )
    places = me * tok + lax.broadcasted_iota(jnp.int32, (tok, 1), 0)
    valid = places < lens[prompt]
    model = key_ref.shape[-1]
    per = model // chunk
    for n in range(per, 3 * per):
        weights = ws[n // blocks, :, (n % blocks) * chunk : (n % blocks + 1) * chunk]
        piece = jnp.dot(normed, weights, preferred_element_type=F32)
        piece = piece + bias[:, n * chunk : (n + 1) * chunk]
        cols = slice((n % per) * chunk, (n % per + 1) * chunk)
        if n < 2 * per:
            piece = turn(piece, cos_ref[...], sin_ref[...])
            key_ref[0, :, cols] = jnp.where(valid, piece, 0.0).astype(BF)
        else:
            value_ref[0, :, cols] = jnp.where(valid, piece, 0.0).astype(BF)


def local(
    prompts,
    perm,
    lengths,
    norm_attn,
    norm_mlp,
    qkv_train,
    qkv_bias,
    out_train,
    gateup_train,
    down_train,
):
    count, tok, width = prompts.shape
    groups = lax.axis_size("seq")
    parts = lax.axis_size("req")
    total = groups * tok
    me = lax.axis_index("seq").astype(jnp.int32)
    req = lax.axis_index("req").astype(jnp.int32)
    share = groups // 2
    heads = HEADS // share
    thirds = count // 2
    bits = [4, 2, 4] if groups == 8 else [share] * thirds
    halves = [lax.rem(lax.div(me, jnp.int32(bit)), jnp.int32(2)) for bit in bits]
    whiches = [lax.div(me, jnp.int32(2 * bit)) * bit + lax.rem(me, jnp.int32(bit)) for bit in bits]
    own_w = heads * HD
    anywhere = pl.BlockSpec(memory_space=pl.ANY)

    normed = rms_scale(prompts, norm_attn).astype(BF)

    info = jnp.stack([req, me])
    smem = pl.BlockSpec(memory_space=pltpu.SMEM)
    bundle = jax.ShapeDtypeStruct((parts, thirds, tok // 2, width), BF)
    packed, color, rank = pl.pallas_call(
        functools.partial(route_kernel, count, thirds),
        out_shape=[
            bundle,
            jax.ShapeDtypeStruct(perm.shape, jnp.int32),
            jax.ShapeDtypeStruct((2 * perm.shape[0],), jnp.int32),
        ],
        in_specs=[smem, smem, pl.BlockSpec(memory_space=pltpu.VMEM)],
        out_specs=[anywhere, smem, smem],
        scratch_shapes=[pltpu.SMEM(perm.shape, jnp.int32), pltpu.SemaphoreType.DMA((2 * count,))],
        name="route",
    )(info, perm, normed.reshape(count, 2, tok // 2, width))

    def forth(packed):
        return lax.all_to_all(packed, "req", split_axis=0, concat_axis=0, tiled=True)

    def sort(got):
        return pl.pallas_call(
            functools.partial(pass_kernel, count, parts),
            out_shape=[jax.ShapeDtypeStruct(bundle.shape[1:], BF)] * parts,
            in_specs=[smem] * 4 + [pl.BlockSpec(memory_space=pltpu.VMEM)],
            out_specs=[anywhere] * parts,
            scratch_shapes=[pltpu.SemaphoreType.DMA(perm.shape)],
            name="sort",
        )(info, perm, color, rank, got)

    def hops_ahead(array, d):
        return lax.ppermute(array, "req", [(i, (i + d) % parts) for i in range(parts)])

    cosine, sine = tables(total)
    chunk = 256
    blocks = qkv_train.shape[1] // chunk

    def attend(j, x_parts, weights):
        n_x, n_w = len(x_parts), len(weights)
        slot = req * count + halves[j] * thirds + j
        info = jnp.concatenate([jnp.stack([req, me, slot, whiches[j]]), relative])
        bias = lax.dynamic_index_in_dim(
            qkv_bias.reshape(3, share, own_w), whiches[j], 1, keepdims=False
        ).reshape(1, 3 * own_w)
        return pl.pallas_call(
            functools.partial(attend_kernel, j, n_x, n_w, tok, heads, chunk, blocks),
            out_shape=jax.ShapeDtypeStruct((total, own_w), BF),
            grid_spec=pltpu.PrefetchScalarGridSpec(
                num_scalar_prefetch=2,
                grid=(1,),
                in_specs=[anywhere] * (n_x + n_w)
                + [
                    pl.BlockSpec((1, 3 * own_w), lambda i, *_: (0, 0)),
                    pl.BlockSpec((total, 128), lambda i, *_: (0, 0)),
                    pl.BlockSpec((total, 128), lambda i, *_: (0, 0)),
                ],
                out_specs=pl.BlockSpec((total, own_w), lambda i, *_: (0, 0)),
                scratch_shapes=[
                    pltpu.VMEM((total, width), BF),
                    pltpu.VMEM((width, 3 * own_w), BF),
                    pltpu.VMEM((heads, total, HD), BF),
                    pltpu.VMEM((heads, total, HD), BF),
                    pltpu.VMEM((heads, total, 128), BF),
                    pltpu.SemaphoreType.DMA((groups + 6 * groups,)),
                ],
            ),
            compiler_params=pltpu.CompilerParams(vmem_limit_bytes=VMEM),
            cost_estimate=pl.CostEstimate(
                flops=1_000_000_000, bytes_accessed=1_000_000, transcendentals=0
            ),
            name="attend",
        )(info, lengths, *x_parts, *weights, bias, cosine, sine)

    def spread_heads(out):
        return lax.all_to_all(
            out.reshape(-1, groups, tok, own_w), "seq", split_axis=1, concat_axis=1, tiled=True
        )

    rows_o = out_train.shape[0]
    qkv = qkv_train.astype(BF)
    gateup = gateup_train.astype(BF)
    tail = jnp.concatenate([out_train.astype(BF), down_train.astype(BF)], axis=0)
    if groups == 8:
        def prompt_of(j, other):
            side = 1 - halves[j] if other else halves[j]
            return lax.dynamic_index_in_dim(normed, side * thirds + j, 0, keepdims=False)

        def halved(array):
            rows = array.shape[1] // 2
            return [array[:, :rows], array[:, rows:]]

        def first_way(held):
            return [*held, swap(held[0], 2), swap(held[1], 4)]

        def second_way(held):
            upper, lower, upper_x, lower_y = held
            upper, lower = jnp.stack([upper, upper_x]), jnp.stack([lower, lower_y])
            return [upper, lower, swap(upper, 4), swap(lower, 2)]

        def both_cores(held):
            return [*held, *(swap(array, 1) for array in held)]

        kinds = [[j for j in range(thirds) if bits[j] == bit] for bit in (4, 2)]
        far = [jnp.stack([prompt_of(j, True) for j in kind]) for kind in kinds]
        near = [jnp.stack([prompt_of(j, False) for j in kind]) for kind in kinds]
        split = qkv.shape[1]
        hops = [jnp.concatenate([qkv, gateup], axis=1)]
        along_y = swap(jnp.concatenate([far[0], near[1]]), 4)
        along_x = swap(jnp.concatenate([far[1], near[0]]), 2)
        for _ in range(parts - 1):
            hops.append(hop(hops[-1]))

        *hops, along_x, along_y, tail, packed = gate([*hops, along_x, along_y, tail, packed])
        qkv_c = jnp.stack([h[:, :split] for h in hops])
        gu_c = jnp.stack([h[:, split:] for h in hops])
        n_y, n_x = len(kinds[0]), len(kinds[1])
        far_x = swap(along_y[:n_y], 2)
        far_y = swap(along_x[:n_x], 4)
        w_at = first_way(halved(qkv_c))
        tails = [tail]
        for _ in range(parts - 1):
            tails.append(hop(tails[-1]))

        far_x, far_y, *held = gate([far_x, far_y, *w_at, *tails, packed])
        w_at, tails, packed = held[:4], held[4:-1], held[-1]
        w_at = second_way(w_at)
        got = forth(packed)
        pieces = [None] * thirds
        for i, j in enumerate(kinds[0]):
            pieces[j] = jnp.stack([near[0][i], along_x[n_x + i], along_y[i], far_x[i]])
        for i, j in enumerate(kinds[1]):
            pieces[j] = jnp.stack([near[1][i], along_x[i], along_y[n_y + i], far_y[i]])
        pieces = jnp.stack(pieces)
        x_parts = [pieces, swap(pieces, 1)]

        *w_at, x_parts[0], x_parts[1], gu_c = gate([*w_at, *x_parts, gu_c])
        qkv_w = both_cores(w_at)
        g_at = first_way(halved(gu_c))
        t_at = first_way(halved(jnp.stack(tails)))

        relative = steps_back()
        out_a = attend(0, x_parts, qkv_w)

        out_a, *held = gate([out_a, *t_at, *g_at])
        t_at, g_at = second_way(held[:4]), held[4:]
        out_b = attend(1, [after(x_parts[0], out_a), x_parts[1]], qkv_w)
        g_at = second_way(g_at)

        out_a, out_b, got, *t_at = gate([out_a, out_b, got, *t_at])
        attended = [spread_heads(jnp.stack([out_a, out_b]))]
        sorted_rows = sort(got)
        across = hops_ahead(sorted_rows[2], 2)
        out = attend(2, [after(x_parts[0], out_b), x_parts[1]], qkv_w)

        out, attended[0], across, *held = gate([out, *attended, across, *g_at, *t_at])
        gu_w, tail_w = both_cores(held[:4]), both_cores(held[4:])
        sorted_rows = gate([*sorted_rows, out])
        arrived = [
            sorted_rows[0], hops_ahead(sorted_rows[1], 1), across, hops_ahead(sorted_rows[3], 3)
        ]
        attended.append(spread_heads(out[None]))
    else:
        relative = jnp.arange(parts, dtype=jnp.int32)
        qkv_c, gu_c, tail_c = (lax.all_gather(w, "req", axis=0) for w in (qkv, gateup, tail))
        qkv_w, gu_w = whole(qkv_c), whole(gu_c)
        tail_w = whole(tail_c[:, :rows_o]) + whole(tail_c[:, rows_o:])
        everything = lax.all_gather(normed, "seq", axis=0)
        sorted_rows = sort(forth(packed))
        arrived = [sorted_rows[0]] + [hops_ahead(sorted_rows[d], d) for d in range(1, parts)]
        if own_w == chunk:
            attend_w = qkv_w
        else:
            full = qkv_w[0][0].transpose(1, 0, 2).reshape(width, 3, share, own_w)
            attend_w = lax.dynamic_index_in_dim(full, whiches[0], 2, keepdims=False)
            attend_w = [attend_w.reshape(1, width, 3 * own_w)]
        outs = []
        for j in range(thirds):
            mine = lax.dynamic_index_in_dim(everything, halves[j] * thirds + j, 1, keepdims=False)
            outs.append(attend(j, [mine], attend_w))
        attended = [spread_heads(jnp.stack(outs))]


    info = jnp.concatenate([jnp.stack([req, me, jnp.int32(0), jnp.int32(0)]), relative])
    n_w = len(gu_w)

    def prompt_at(i, *_):
        return (lax.rem(i, 2) * thirds + lax.div(i, 2), 0, 0)

    states = pl.pallas_call(
        functools.partial(mlp_kernel, n_w, tok, bits, [a.shape[0] for a in attended]),
        out_shape=jax.ShapeDtypeStruct((count, tok, width), BF),
        grid_spec=pltpu.PrefetchScalarGridSpec(
            num_scalar_prefetch=2,
            grid=(count,),
            in_specs=[pl.BlockSpec((1, tok, width), prompt_at)]
            + [anywhere] * (len(attended) + n_w + len(tail_w))
            + [pl.BlockSpec((1, width), lambda i, *_: (0, 0))],
            out_specs=pl.BlockSpec((1, tok, width), prompt_at),
            scratch_shapes=[
                pltpu.VMEM((thirds, groups, tok, own_w), BF),
                pltpu.VMEM((parts, width, out_train.shape[1]), BF),
                pltpu.VMEM((parts, width, gateup_train.shape[1]), BF),
                pltpu.VMEM((parts, groups * down_train.shape[0], down_train.shape[1]), BF),
                pltpu.SemaphoreType.DMA((thirds + 6 * groups * parts,)),
            ],
        ),
        compiler_params=pltpu.CompilerParams(vmem_limit_bytes=VMEM),
        cost_estimate=pl.CostEstimate(
            flops=1_000_000_000, bytes_accessed=1_000_000, transcendentals=0
        ),
        name="feed_forward",
    )(info, lengths, prompts, *attended, *gu_w, *tail_w, norm_mlp.reshape(1, width))

    own_rows = pl.BlockSpec((tok, 128), lambda i, info, *_: (info[1], 0))
    n_w = len(qkv_w)
    keys, values = pl.pallas_call(
        functools.partial(cache_kernel, n_w, tok, chunk, blocks),
        out_shape=[jax.ShapeDtypeStruct((count, tok, width), BF)] * 2,
        grid_spec=pltpu.PrefetchScalarGridSpec(
            num_scalar_prefetch=5,
            grid=(count,),
            in_specs=[anywhere] * n_w
            + [
                pl.BlockSpec((1, 3 * width), lambda i, *_: (0, 0)),
                own_rows,
                own_rows,
            ]
            + [anywhere] * parts,
            out_specs=[pl.BlockSpec((1, tok, width), lambda i, *_: (i, 0, 0))] * 2,
            scratch_shapes=[
                pltpu.VMEM((parts, width, qkv_train.shape[1]), BF),
                pltpu.VMEM(bundle.shape, BF),
                pltpu.SemaphoreType.DMA((2 * groups * parts + parts,)),
            ],
        ),
        compiler_params=pltpu.CompilerParams(vmem_limit_bytes=VMEM),
        cost_estimate=pl.CostEstimate(
            flops=1_000_000_000, bytes_accessed=1_000_000, transcendentals=0
        ),
        name="caches",
    )(after(info, states), perm, lengths, color, rank, *qkv_w, qkv_bias.reshape(1, 3 * width), cosine, sine, *arrived)
    return (states, keys, values)


def solution(mesh):
    placed = (
        P("req", "seq", None),
        P(),
        P(),
        P(),
        P(),
        P("seq", "req"),
        P(),
        P("seq", "req"),
        P("seq", "req"),
        P("seq", "req"),
    )
    return jax.shard_map(
        local,
        mesh=mesh,
        in_specs=placed,
        out_specs=(P("req", "seq", None), P("req", "seq", None), P("req", "seq", None)),
        check_vma=False,
    )
```

```python
import functools

import jax
import jax.numpy as jnp
import numpy as np
from jax import lax
from jax.experimental import pallas as pl
from jax.experimental.pallas import tpu as pltpu
from jax.sharding import PartitionSpec as P

HEADS = 16
HD = 64
BF = jnp.bfloat16
F32 = jnp.float32
LOG2E = 1.4426950408889634
VMEM = 60 * 1024 * 1024
MASKS = (0, 2, 4, 6)
PAIRS = (((0, 2), 0), ((0, 4), 1), ((4, 6), 0), ((2, 6), 1))


def rms_scale(rows, gain):
    rows = rows.astype(F32)
    return rows * lax.rsqrt(jnp.mean(rows * rows, axis=-1, keepdims=True) + 1e-06) * gain


def swap(array, mask):
    groups = lax.axis_size("seq")
    return lax.ppermute(array, "seq", [(i, i ^ mask) for i in range(groups)])


def after(array, *others):
    return lax.optimization_barrier((array, *others))[0]


def whole(array):
    return [lax.all_gather(array, "seq", axis=1, tiled=True)[None]]


def ring_order():
    parts = lax.axis_size("req")
    return list(range(1, parts, 2)) + list(range(0, parts, 2))[::-1]


def hop(array):
    order = ring_order()
    return lax.ppermute(
        array, "req", [(order[i], order[(i + 1) % len(order)]) for i in range(len(order))]
    )


def steps_back():
    order = ring_order()
    place = np.argsort(np.array(order)).astype(np.int32)
    here = jnp.take(jnp.asarray(place), lax.axis_index("req"))
    return lax.rem(here - place + np.int32(len(order)), jnp.int32(len(order)))


def gate(held):
    return lax.optimization_barrier(tuple(held))


def sources(refs, me):
    rows = refs[0].shape[-2]
    if len(refs) == 1:
        return [(refs[0].at[g], g * rows, g) for g in range(refs[0].shape[0])]
    found = []
    half = len(refs) // 2
    for n, ref in enumerate(refs):
        core = n // half
        masks, part = (MASKS, 0) if half == 1 else PAIRS[n % half]
        parts = 1 if half == 1 else 2
        for i, mask in enumerate(masks):
            whose = jnp.bitwise_xor(me, mask ^ core)
            found.append((ref.at[i], pl.multiple_of((whose * parts + part) * rows, rows), part))
    return found


def tables(length):
    half = HD // 2
    freqs = np.power(1000000.0, -2.0 * np.arange(half) / HD)
    angle = np.arange(length)[:, None] * freqs[None, :]
    cosine = np.cos(angle).astype(np.float32)
    sine = np.sin(angle).astype(np.float32)
    return (
        jnp.asarray(np.concatenate([cosine] * (128 // half), axis=1)),
        jnp.asarray(np.concatenate([-sine, sine] * (64 // half), axis=1)),
    )


def turn(block, cosine, sine):
    rows, width = block.shape
    half = HD // 2
    if width < 128:
        cosine, sine = cosine[:, :width], sine[:, :width]
    elif width > 128:
        cosine = jnp.concatenate([cosine] * (width // 128), axis=1)
        sine = jnp.concatenate([sine] * (width // 128), axis=1)
    if width < 128:
        other = jnp.concatenate([block[:, half:], block[:, :half]], axis=1)
    else:
        lane = lax.broadcasted_iota(jnp.int32, block.shape, 1)
        low = (lane % HD) < half
        other = jnp.where(low, pltpu.roll(block, width - half, 1), pltpu.roll(block, half, 1))
    return block * cosine + other * sine


def attend_kernel(j, count, count_w, tok, heads, chunk, blocks, info, lens, *refs):
    x_refs, refs = refs[:count], refs[count:]
    w_refs, refs = refs[:count_w], refs[count_w:]
    if count > 1:
        x_refs = [ref.at[j] for ref in x_refs]
    bias, cos_ref, sin_ref, out_ref, xs, ws, qs, ks, vs, sems = refs
    me = info[1]
    slot = info[2]
    length = lens[slot]
    total = xs.shape[0]
    groups = total // tok
    blk = min(256, total)
    width = heads * HD
    rows_w = w_refs[0].shape[-2]
    which = info[3]
    copies = []

    def copy_of(source, target):
        copies.append(pltpu.make_async_copy(source, target, sems.at[len(copies)]))

    for ref, at, _ in sources(x_refs, me):
        copy_of(ref, xs.at[pl.ds(at, tok), :])
    for ref, at, _ in sources(w_refs, me):
        place = pl.ds(at, rows_w)
        if chunk == width:
            for part in range(3):
                n = part * (HEADS // heads) + which
                k = info[4 + lax.div(n, blocks)]
                off = pl.multiple_of(lax.rem(n, blocks) * chunk, chunk)
                copy_of(
                    ref.at[k, :, pl.ds(off, chunk)], ws.at[place, pl.ds(part * width, width)]
                )
        else:
            copy_of(ref, ws.at[place, :])
    for copy in copies:
        copy.start()
    ones = jnp.where(
        lax.broadcasted_iota(jnp.int32, (blk, 128 - HD), 1) == 0, 1.0, 0.0
    ).astype(BF)
    for copy in copies:
        copy.wait()
    steps = lax.div(length + (blk - 1), blk)

    def project(i, carry):
        place = pl.ds(pl.multiple_of(i * blk, blk), blk)
        qkv = jnp.dot(xs[place, :], ws[...], preferred_element_type=F32) + bias[...]
        cosine, sine = cos_ref[place, :], sin_ref[place, :]
        query = turn(qkv[:, :width], cosine, sine).astype(BF)
        keys = turn(qkv[:, width : 2 * width], cosine, sine).astype(BF)
        values = qkv[:, 2 * width :].astype(BF)
        for h in range(heads):
            cols = slice(h * HD, (h + 1) * HD)
            qs[h, place, :] = query[:, cols]
            ks[h, place, :] = keys[:, cols]
            vs[h, place, :] = jnp.concatenate([values[:, cols], ones], axis=1)
        return carry

    lax.fori_loop(0, steps, project, 0)
    causal = lax.broadcasted_iota(jnp.int32, (blk, blk), 1) <= lax.broadcasted_iota(
        jnp.int32, (blk, blk), 0
    )
    factor = HD ** (-0.5) * LOG2E
    for i in range(total // blk):
        span = (i + 1) * blk
        place = slice(i * blk, span)

        @pl.when(i * blk < length)
        def _():
            for h in range(heads):
                scores = lax.dot_general(
                    qs[h, place, :],
                    ks[h, :span, :],
                    (((1,), (1,)), ((), ())),
                    preferred_element_type=F32,
                )
                last = jnp.where(causal, scores[:, i * blk :], -1e30)
                if i:
                    scores = jnp.concatenate([scores[:, : i * blk], last], axis=1)
                else:
                    scores = last
                top = jnp.max(scores, axis=-1, keepdims=True)
                expo = jnp.exp2((scores - top) * factor).astype(BF)
                mixed = jnp.dot(expo, vs[h, :span, :], preferred_element_type=F32)
                out_ref[place, h * HD : (h + 1) * HD] = (
                    mixed[:, :HD] / mixed[:, HD : HD + 1]
                ).astype(BF)

        @pl.when(i * blk >= length)
        def _():
            out_ref[place, :] = jnp.zeros((blk, width), BF)


def mlp_kernel(count, tok, bits, chunks, info, lens, *refs):
    x_ref, refs = refs[0], refs[1:]
    thirds = x_ref.shape[0]
    a_refs, refs = refs[: len(chunks)], refs[len(chunks) :]
    gu_refs, refs = refs[:count], refs[count:]
    if count == 1:
        out_refs, down_refs, refs = refs[:1], refs[1:2], refs[2:]
    else:
        tail_refs, refs = refs[:count], refs[count:]
    gain, states, att, wo, wg, wd, sems = refs
    req, me = info[0], info[1]
    step = pl.program_id(0)
    groups = att.shape[1]
    blocks = wo.shape[0]

    def pick(items, dest, first):
        return [
            pltpu.make_async_copy(
                ref.at[info[4 + k], pl.ds(start, rows), :],
                dest.at[k, pl.ds(at, rows), :],
                sems.at[first + i * blocks + k],
            )
            for i, (ref, start, at, rows) in enumerate(items)
            for k in range(blocks)
        ]

    def pieces(refs):
        rows = refs[0].shape[-2]
        return [(ref, 0, at, rows) for ref, at, _ in sources(refs, me)]

    def tail_pieces(down):
        rows_o, rows_d = wo.shape[1] // groups, wd.shape[1] // groups
        rows = tail_refs[0].shape[-2]
        items = []
        for ref, at, part in sources(tail_refs, me):
            low, high = part * rows, (part + 1) * rows
            start = max(low, rows_o) if down else low
            stop = high if down else min(high, rows_o)
            if start < stop:
                skip, size = (rows_o, rows_d) if down else (0, rows_o)
                whose = lax.div(at, 2 * rows)
                at = pl.multiple_of(whose * size + (start - skip), 16)
                items.append((ref, start - low, at, stop - start))
        return items

    def load(index):
        first = thirds + index * 2 * groups * blocks
        if index == 1:
            return pick(pieces(gu_refs), wg, first)
        dest = wd if index else wo
        if count == 1:
            items = pieces(down_refs if index else out_refs)
        else:
            items = tail_pieces(index == 2)
        copies = pick(items, dest, first)
        if index == 0:
            copies += [
                pltpu.make_async_copy(
                    ref, att.at[pl.ds(sum(chunks[:i]), chunks[i])], sems.at[i]
                )
                for i, ref in enumerate(a_refs)
            ]
        return copies

    def arrive(index):
        @pl.when(step == 0)
        def _():
            for copy in load(index):
                copy.wait()

    @pl.when(step == 0)
    def _():
        for index in range(3):
            for copy in load(index):
                copy.start()

    arrive(0)
    share = groups // 2
    attended = jnp.concatenate(
        [
            jnp.concatenate(
                [att[j, (h // bit * 2 + step) * bit + h % bit] for h in range(share)], axis=1
            )
            for j, bit in enumerate(bits)
        ],
        axis=0,
    )
    rows = x_ref[...].reshape(thirds * tok, x_ref.shape[2]).astype(F32)
    mid = rows + jnp.concatenate(
        [jnp.dot(attended, wo[k], preferred_element_type=F32) for k in range(blocks)], axis=1
    )
    normed = rms_scale(mid, gain[...]).astype(BF)
    arrive(1)
    hidden = []
    for k in range(blocks // 2):
        gate = jnp.dot(normed, wg[k], preferred_element_type=F32)
        up = jnp.dot(normed, wg[k + blocks // 2], preferred_element_type=F32)
        hidden.append((gate * jax.nn.sigmoid(gate) * up).astype(BF))
    hidden = jnp.concatenate(hidden, axis=1)
    arrive(2)
    final = mid + jnp.concatenate(
        [jnp.dot(hidden, wd[k], preferred_element_type=F32) for k in range(blocks)], axis=1
    )
    places = me * tok + lax.broadcasted_iota(jnp.int32, (tok, 1), 0)
    for j in range(thirds):
        length = lens[(req * 2 + step) * thirds + j]
        mine = final[j * tok : (j + 1) * tok]
        states[j] = jnp.where(places < length, mine, 0.0).astype(BF)


def cache_kernel(count, tok, chunk, blocks, info, perm, lens, x_ref, *refs):
    w_refs, refs = refs[:count], refs[count:]
    bias, cos_ref, sin_ref, key_ref, value_ref, ws, sems = refs
    req, me = info[0], info[1]
    step = pl.program_id(0)
    size = pl.num_programs(0)
    rows = w_refs[0].shape[-2]

    @pl.when(step == 0)
    def _():
        copies = [
            pltpu.make_async_copy(
                ref.at[info[4 + k]], ws.at[k, pl.ds(at, rows), :], sems.at[i * ws.shape[0] + k]
            )
            for i, (ref, at, _) in enumerate(sources(w_refs, me))
            for k in range(ws.shape[0])
        ]
        for copy in copies:
            copy.start()
        for copy in copies:
            copy.wait()

    normed = x_ref[0]
    places = me * tok + lax.broadcasted_iota(jnp.int32, (tok, 1), 0)
    valid = places < lens[perm[req * size + step]]
    model = key_ref.shape[-1]
    per = model // chunk
    for n in range(per, 3 * per):
        weights = ws[n // blocks, :, (n % blocks) * chunk : (n % blocks + 1) * chunk]
        piece = jnp.dot(normed, weights, preferred_element_type=F32)
        piece = piece + bias[:, n * chunk : (n + 1) * chunk]
        cols = slice((n % per) * chunk, (n % per + 1) * chunk)
        if n < 2 * per:
            piece = turn(piece, cos_ref[...], sin_ref[...])
            key_ref[0, :, cols] = jnp.where(valid, piece, 0.0).astype(BF)
        else:
            value_ref[0, :, cols] = jnp.where(valid, piece, 0.0).astype(BF)


def local(
    prompts,
    perm,
    lengths,
    norm_attn,
    norm_mlp,
    qkv_train,
    qkv_bias,
    out_train,
    gateup_train,
    down_train,
):
    count, tok, width = prompts.shape
    groups = lax.axis_size("seq")
    parts = lax.axis_size("req")
    total = groups * tok
    me = lax.axis_index("seq").astype(jnp.int32)
    req = lax.axis_index("req").astype(jnp.int32)
    share = groups // 2
    heads = HEADS // share
    thirds = count // 2
    bits = [4, 2, 4] if groups == 8 else [share] * thirds
    halves = [lax.rem(lax.div(me, jnp.int32(bit)), jnp.int32(2)) for bit in bits]
    whiches = [lax.div(me, jnp.int32(2 * bit)) * bit + lax.rem(me, jnp.int32(bit)) for bit in bits]
    own_w = heads * HD
    anywhere = pl.BlockSpec(memory_space=pl.ANY)

    normed = rms_scale(prompts, norm_attn).astype(BF)

    cosine, sine = tables(total)
    chunk = 256
    blocks = qkv_train.shape[1] // chunk

    def attend(j, x_parts, weights):
        n_x, n_w = len(x_parts), len(weights)
        slot = req * count + halves[j] * thirds + j
        info = jnp.concatenate([jnp.stack([req, me, slot, whiches[j]]), relative])
        bias = lax.dynamic_index_in_dim(
            qkv_bias.reshape(3, share, own_w), whiches[j], 1, keepdims=False
        ).reshape(1, 3 * own_w)
        return pl.pallas_call(
            functools.partial(attend_kernel, j, n_x, n_w, tok, heads, chunk, blocks),
            out_shape=jax.ShapeDtypeStruct((total, own_w), BF),
            grid_spec=pltpu.PrefetchScalarGridSpec(
                num_scalar_prefetch=2,
                grid=(1,),
                in_specs=[anywhere] * (n_x + n_w)
                + [
                    pl.BlockSpec((1, 3 * own_w), lambda i, *_: (0, 0)),
                    pl.BlockSpec((total, 128), lambda i, *_: (0, 0)),
                    pl.BlockSpec((total, 128), lambda i, *_: (0, 0)),
                ],
                out_specs=pl.BlockSpec((total, own_w), lambda i, *_: (0, 0)),
                scratch_shapes=[
                    pltpu.VMEM((total, width), BF),
                    pltpu.VMEM((width, 3 * own_w), BF),
                    pltpu.VMEM((heads, total, HD), BF),
                    pltpu.VMEM((heads, total, HD), BF),
                    pltpu.VMEM((heads, total, 128), BF),
                    pltpu.SemaphoreType.DMA((groups + 6 * groups,)),
                ],
            ),
            compiler_params=pltpu.CompilerParams(vmem_limit_bytes=VMEM),
            cost_estimate=pl.CostEstimate(
                flops=1_000_000_000, bytes_accessed=1_000_000, transcendentals=0
            ),
            name="attend",
        )(info, lengths, *x_parts, *weights, bias, cosine, sine)

    def spread_heads(out):
        return lax.all_to_all(
            out.reshape(1, groups, tok, own_w), "seq", split_axis=1, concat_axis=1, tiled=True
        )

    rows_o = out_train.shape[0]
    qkv = qkv_train.astype(BF)
    gateup = gateup_train.astype(BF)
    tail = jnp.concatenate([out_train.astype(BF), down_train.astype(BF)], axis=0)
    if groups == 8:
        def prompt_of(j, other):
            side = 1 - halves[j] if other else halves[j]
            return lax.dynamic_index_in_dim(normed, side * thirds + j, 0, keepdims=False)

        def halved(array):
            rows = array.shape[1] // 2
            return [array[:, :rows], array[:, rows:]]

        def first_way(held):
            return [*held, swap(held[0], 2), swap(held[1], 4)]

        def second_way(held):
            upper, lower, upper_x, lower_y = held
            upper, lower = jnp.stack([upper, upper_x]), jnp.stack([lower, lower_y])
            return [upper, lower, swap(upper, 4), swap(lower, 2)]

        def both_cores(held):
            return [*held, *(swap(array, 1) for array in held)]

        kinds = [[j for j in range(thirds) if bits[j] == bit] for bit in (4, 2)]
        far = [jnp.stack([prompt_of(j, True) for j in kind]) for kind in kinds]
        near = [jnp.stack([prompt_of(j, False) for j in kind]) for kind in kinds]
        along_y = swap(jnp.concatenate([far[0], near[1]]), 4)
        along_x = swap(jnp.concatenate([far[1], near[0]]), 2)

        def round_trip(array):
            held = [array]
            for _ in range(parts - 1):
                held.append(hop(held[-1]))
            return held

        qkv_hops = round_trip(after(qkv, normed))
        gu_hops = round_trip(after(gateup, qkv_hops[1]))

        *qkv_hops, along_x, along_y, gu_hops[2], tail = gate(
            [*qkv_hops, along_x, along_y, gu_hops[2], tail]
        )
        qkv_c = jnp.stack(qkv_hops)
        gu_hops[3] = hop(gu_hops[2])
        n_y, n_x = len(kinds[0]), len(kinds[1])
        far_x = swap(along_y[:n_y], 2)
        far_y = swap(along_x[:n_x], 4)
        w_at = first_way(halved(qkv_c))
        tails = round_trip(after(tail, gu_hops[3]))
        gu_c = jnp.stack(gu_hops)

        far_x, far_y, *held = gate([far_x, far_y, *w_at, *tails])
        w_at, tails = held[:4], held[4:]
        w_at = second_way(w_at)
        to_caches = after(normed, tails[-1])
        pieces = [None] * thirds
        for i, j in enumerate(kinds[0]):
            pieces[j] = jnp.stack([near[0][i], along_x[n_x + i], along_y[i], far_x[i]])
        for i, j in enumerate(kinds[1]):
            pieces[j] = jnp.stack([near[1][i], along_x[i], along_y[n_y + i], far_y[i]])
        pieces = jnp.stack(pieces)
        x_parts = [pieces, swap(pieces, 1)]

        *w_at, x_parts[0], x_parts[1], gu_c = gate([*w_at, *x_parts, gu_c])
        qkv_w = both_cores(w_at)
        g_at = first_way(halved(gu_c))
        t_at = first_way(halved(jnp.stack(tails)))

        relative = steps_back()
        out = attend(0, x_parts, qkv_w)

        out, *held = gate([out, *t_at, *g_at])
        attended = [spread_heads(out)]

        t_at, g_at = second_way(held[:4]), held[4:]
        out = attend(1, [after(x_parts[0], out), x_parts[1]], qkv_w)

        out, attended[0], *held = gate([out, attended[0], *t_at, *g_at])
        attended.append(spread_heads(out))
        g_at, tail_w = second_way(held[4:]), both_cores(held[:4])
        out = attend(2, [after(x_parts[0], out), x_parts[1]], qkv_w)

        out, attended[1], *held = gate([out, attended[1], *g_at, *tail_w])
        attended.append(spread_heads(out))
        gu_w, tail_w = both_cores(held[:4]), held[4:]
    else:
        relative = jnp.arange(parts, dtype=jnp.int32)
        qkv_c, gu_c, tail_c = (lax.all_gather(w, "req", axis=0) for w in (qkv, gateup, tail))
        qkv_w, gu_w = whole(qkv_c), whole(gu_c)
        tail_w = whole(tail_c[:, :rows_o]) + whole(tail_c[:, rows_o:])
        everything = lax.all_gather(normed, "seq", axis=0)
        to_caches = normed
        if own_w == chunk:
            attend_w = qkv_w
        else:
            full = qkv_w[0][0].transpose(1, 0, 2).reshape(width, 3, share, own_w)
            attend_w = lax.dynamic_index_in_dim(full, whiches[0], 2, keepdims=False)
            attend_w = [attend_w.reshape(1, width, 3 * own_w)]
        outs = []
        for j in range(thirds):
            mine = lax.dynamic_index_in_dim(everything, halves[j] * thirds + j, 1, keepdims=False)
            outs.append(attend(j, [mine], attend_w))
        attended = [spread_heads(out) for out in outs]


    info = jnp.concatenate([jnp.stack([req, me, jnp.int32(0), jnp.int32(0)]), relative])
    n_w = len(gu_w)

    third = pl.BlockSpec((thirds, tok, width), lambda i, *_: (i, 0, 0))
    states = pl.pallas_call(
        functools.partial(mlp_kernel, n_w, tok, bits, [a.shape[0] for a in attended]),
        out_shape=jax.ShapeDtypeStruct((count, tok, width), BF),
        grid_spec=pltpu.PrefetchScalarGridSpec(
            num_scalar_prefetch=2,
            grid=(2,),
            in_specs=[third]
            + [anywhere] * (len(attended) + n_w + len(tail_w))
            + [pl.BlockSpec((1, width), lambda i, *_: (0, 0))],
            out_specs=third,
            scratch_shapes=[
                pltpu.VMEM((thirds, groups, tok, own_w), BF),
                pltpu.VMEM((parts, width, out_train.shape[1]), BF),
                pltpu.VMEM((parts, width, gateup_train.shape[1]), BF),
                pltpu.VMEM((parts, groups * down_train.shape[0], down_train.shape[1]), BF),
                pltpu.SemaphoreType.DMA((thirds + 6 * groups * parts,)),
            ],
        ),
        compiler_params=pltpu.CompilerParams(vmem_limit_bytes=VMEM),
        cost_estimate=pl.CostEstimate(
            flops=1_000_000_000, bytes_accessed=1_000_000, transcendentals=0
        ),
        name="feed_forward",
    )(info, lengths, prompts, *attended, *gu_w, *tail_w, norm_mlp.reshape(1, width))

    everyone = lax.all_gather(to_caches, "req", axis=0, tiled=True)
    own_rows = pl.BlockSpec((tok, 128), lambda i, info, *_: (info[1], 0))
    n_w = len(qkv_w)
    keys, values = pl.pallas_call(
        functools.partial(cache_kernel, n_w, tok, chunk, blocks),
        out_shape=[jax.ShapeDtypeStruct((count, tok, width), BF)] * 2,
        grid_spec=pltpu.PrefetchScalarGridSpec(
            num_scalar_prefetch=3,
            grid=(count,),
            in_specs=[
                pl.BlockSpec(
                    (1, tok, width), lambda i, info, perm, lens: (perm[info[0] * count + i], 0, 0)
                )
            ]
            + [anywhere] * n_w
            + [
                pl.BlockSpec((1, 3 * width), lambda i, *_: (0, 0)),
                own_rows,
                own_rows,
            ],
            out_specs=[pl.BlockSpec((1, tok, width), lambda i, *_: (i, 0, 0))] * 2,
            scratch_shapes=[
                pltpu.VMEM((parts, width, qkv_train.shape[1]), BF),
                pltpu.SemaphoreType.DMA((2 * groups * parts,)),
            ],
        ),
        compiler_params=pltpu.CompilerParams(vmem_limit_bytes=VMEM),
        cost_estimate=pl.CostEstimate(
            flops=1_000_000_000, bytes_accessed=1_000_000, transcendentals=0
        ),
        name="caches",
    )(after(info, states), perm, lengths, everyone, *qkv_w, qkv_bias.reshape(1, 3 * width), cosine, sine)
    return (states, keys, values)


def solution(mesh):
    placed = (
        P("req", "seq", None),
        P(),
        P(),
        P(),
        P(),
        P("seq", "req"),
        P(),
        P("seq", "req"),
        P("seq", "req"),
        P("seq", "req"),
    )
    return jax.shard_map(
        local,
        mesh=mesh,
        in_specs=placed,
        out_specs=(P("req", "seq", None), P("req", "seq", None), P("req", "seq", None)),
        check_vma=False,
    )
```

```python
import functools

import jax
import jax.numpy as jnp
import numpy as np
from jax import lax
from jax.experimental import pallas as pl
from jax.experimental.pallas import tpu as pltpu
from jax.sharding import PartitionSpec as P

HEADS = 16
HD = 64
BF = jnp.bfloat16
F32 = jnp.float32
LOG2E = 1.4426950408889634
VMEM = 60 * 1024 * 1024
MASKS = (0, 2, 4, 6)
PAIRS = (((0, 2), 0), ((0, 4), 1), ((4, 6), 0), ((2, 6), 1))


def rms_scale(rows, gain):
    rows = rows.astype(F32)
    return rows * lax.rsqrt(jnp.mean(rows * rows, axis=-1, keepdims=True) + 1e-06) * gain


def swap(array, mask):
    groups = lax.axis_size("seq")
    return lax.ppermute(array, "seq", [(i, i ^ mask) for i in range(groups)])


def after(array, *others):
    return lax.optimization_barrier((array, *others))[0]


def whole(array):
    return [lax.all_gather(array, "seq", axis=1, tiled=True)[None]]


def ring_order():
    parts = lax.axis_size("req")
    return list(range(1, parts, 2)) + list(range(0, parts, 2))[::-1]


def hop(array):
    order = ring_order()
    return lax.ppermute(
        array, "req", [(order[i], order[(i + 1) % len(order)]) for i in range(len(order))]
    )


def steps_back():
    order = ring_order()
    place = np.argsort(np.array(order)).astype(np.int32)
    here = jnp.take(jnp.asarray(place), lax.axis_index("req"))
    return lax.rem(here - place + np.int32(len(order)), jnp.int32(len(order)))


def gate(held):
    return lax.optimization_barrier(tuple(held))


def sources(refs, me):
    rows = refs[0].shape[-2]
    if len(refs) == 1:
        return [(refs[0].at[g], g * rows, g) for g in range(refs[0].shape[0])]
    found = []
    half = len(refs) // 2
    for n, ref in enumerate(refs):
        core = n // half
        masks, part = (MASKS, 0) if half == 1 else PAIRS[n % half]
        parts = 1 if half == 1 else 2
        for i, mask in enumerate(masks):
            whose = jnp.bitwise_xor(me, mask ^ core)
            found.append((ref.at[i], pl.multiple_of((whose * parts + part) * rows, rows), part))
    return found


def tables(length):
    half = HD // 2
    freqs = np.power(1000000.0, -2.0 * np.arange(half) / HD)
    angle = np.arange(length)[:, None] * freqs[None, :]
    cosine = np.cos(angle).astype(np.float32)
    sine = np.sin(angle).astype(np.float32)
    return (
        jnp.asarray(np.concatenate([cosine] * (128 // half), axis=1)),
        jnp.asarray(np.concatenate([-sine, sine] * (64 // half), axis=1)),
    )


def turn(block, cosine, sine):
    rows, width = block.shape
    half = HD // 2
    if width < 128:
        cosine, sine = cosine[:, :width], sine[:, :width]
    elif width > 128:
        cosine = jnp.concatenate([cosine] * (width // 128), axis=1)
        sine = jnp.concatenate([sine] * (width // 128), axis=1)
    if width < 128:
        other = jnp.concatenate([block[:, half:], block[:, :half]], axis=1)
    else:
        lane = lax.broadcasted_iota(jnp.int32, block.shape, 1)
        low = (lane % HD) < half
        other = jnp.where(low, pltpu.roll(block, width - half, 1), pltpu.roll(block, half, 1))
    return block * cosine + other * sine


def attend_kernel(j, count, count_w, tok, heads, chunk, blocks, info, lens, *refs):
    x_refs, refs = refs[:count], refs[count:]
    w_refs, refs = refs[:count_w], refs[count_w:]
    if count > 1:
        x_refs = [ref.at[j] for ref in x_refs]
    bias, cos_ref, sin_ref, out_ref, xs, ws, qs, ks, vs, sems = refs
    me = info[1]
    slot = info[2]
    length = lens[slot]
    total = xs.shape[0]
    groups = total // tok
    blk = min(256, total)
    width = heads * HD
    rows_w = w_refs[0].shape[-2]
    which = info[3]
    copies = []

    def copy_of(source, target):
        copies.append(pltpu.make_async_copy(source, target, sems.at[len(copies)]))

    for ref, at, _ in sources(x_refs, me):
        copy_of(ref, xs.at[pl.ds(at, tok), :])
    for ref, at, _ in sources(w_refs, me):
        place = pl.ds(at, rows_w)
        if chunk == width:
            for part in range(3):
                n = part * (HEADS // heads) + which
                k = info[4 + lax.div(n, blocks)]
                off = pl.multiple_of(lax.rem(n, blocks) * chunk, chunk)
                copy_of(
                    ref.at[k, :, pl.ds(off, chunk)], ws.at[place, pl.ds(part * width, width)]
                )
        else:
            copy_of(ref, ws.at[place, :])
    for copy in copies:
        copy.start()
    ones = jnp.where(
        lax.broadcasted_iota(jnp.int32, (blk, 128 - HD), 1) == 0, 1.0, 0.0
    ).astype(BF)
    for copy in copies:
        copy.wait()
    steps = lax.div(length + (blk - 1), blk)

    def project(i, carry):
        place = pl.ds(pl.multiple_of(i * blk, blk), blk)
        qkv = jnp.dot(xs[place, :], ws[...], preferred_element_type=F32) + bias[...]
        cosine, sine = cos_ref[place, :], sin_ref[place, :]
        query = turn(qkv[:, :width], cosine, sine).astype(BF)
        keys = turn(qkv[:, width : 2 * width], cosine, sine).astype(BF)
        values = qkv[:, 2 * width :].astype(BF)
        for h in range(heads):
            cols = slice(h * HD, (h + 1) * HD)
            qs[h, place, :] = query[:, cols]
            ks[h, place, :] = keys[:, cols]
            vs[h, place, :] = jnp.concatenate([values[:, cols], ones], axis=1)
        return carry

    lax.fori_loop(0, steps, project, 0)
    causal = lax.broadcasted_iota(jnp.int32, (blk, blk), 1) <= lax.broadcasted_iota(
        jnp.int32, (blk, blk), 0
    )
    factor = HD ** (-0.5) * LOG2E
    for i in range(total // blk):
        span = (i + 1) * blk
        place = slice(i * blk, span)

        @pl.when(i * blk < length)
        def _():
            def score(h):
                return lax.dot_general(
                    qs[h, place, :],
                    ks[h, :span, :],
                    (((1,), (1,)), ((), ())),
                    preferred_element_type=F32,
                )

            following = score(0)
            for h in range(heads):
                scores = following
                if h + 1 < heads:
                    following = score(h + 1)
                last = jnp.where(causal, scores[:, i * blk :], -1e30)
                if i:
                    scores = jnp.concatenate([scores[:, : i * blk], last], axis=1)
                else:
                    scores = last
                top = jnp.max(scores, axis=-1, keepdims=True)
                expo = jnp.exp2((scores - top) * factor).astype(BF)
                mixed = jnp.dot(expo, vs[h, :span, :], preferred_element_type=F32)
                out_ref[place, h * HD : (h + 1) * HD] = (
                    mixed[:, :HD] / mixed[:, HD : HD + 1]
                ).astype(BF)

        @pl.when(i * blk >= length)
        def _():
            out_ref[place, :] = jnp.zeros((blk, width), BF)


def mlp_kernel(count, tok, bits, chunks, info, lens, *refs):
    x_ref, refs = refs[0], refs[1:]
    thirds = x_ref.shape[0]
    a_refs, refs = refs[: len(chunks)], refs[len(chunks) :]
    gu_refs, refs = refs[:count], refs[count:]
    if count == 1:
        out_refs, down_refs, refs = refs[:1], refs[1:2], refs[2:]
    else:
        tail_refs, refs = refs[:count], refs[count:]
    gain, states, att, wo, wg, wd, sems = refs
    req, me = info[0], info[1]
    step = pl.program_id(0)
    groups = att.shape[1]
    blocks = wo.shape[0]

    def pick(items, dest, first):
        return [
            pltpu.make_async_copy(
                ref.at[info[4 + k], pl.ds(start, rows), :],
                dest.at[k, pl.ds(at, rows), :],
                sems.at[first + i * blocks + k],
            )
            for i, (ref, start, at, rows) in enumerate(items)
            for k in range(blocks)
        ]

    def pieces(refs):
        rows = refs[0].shape[-2]
        return [(ref, 0, at, rows) for ref, at, _ in sources(refs, me)]

    def tail_pieces(down):
        rows_o, rows_d = wo.shape[1] // groups, wd.shape[1] // groups
        rows = tail_refs[0].shape[-2]
        items = []
        for ref, at, part in sources(tail_refs, me):
            low, high = part * rows, (part + 1) * rows
            start = max(low, rows_o) if down else low
            stop = high if down else min(high, rows_o)
            if start < stop:
                skip, size = (rows_o, rows_d) if down else (0, rows_o)
                whose = lax.div(at, 2 * rows)
                at = pl.multiple_of(whose * size + (start - skip), 16)
                items.append((ref, start - low, at, stop - start))
        return items

    def load(index):
        first = thirds + index * 2 * groups * blocks
        if index == 1:
            return pick(pieces(gu_refs), wg, first)
        dest = wd if index else wo
        if count == 1:
            items = pieces(down_refs if index else out_refs)
        else:
            items = tail_pieces(index == 2)
        copies = pick(items, dest, first)
        if index == 0:
            copies += [
                pltpu.make_async_copy(
                    ref, att.at[pl.ds(sum(chunks[:i]), chunks[i])], sems.at[i]
                )
                for i, ref in enumerate(a_refs)
            ]
        return copies

    def arrive(index):
        @pl.when(step == 0)
        def _():
            for copy in load(index):
                copy.wait()

    @pl.when(step == 0)
    def _():
        for index in range(3):
            for copy in load(index):
                copy.start()

    arrive(0)
    share = groups // 2
    attended = jnp.concatenate(
        [
            jnp.concatenate(
                [att[j, (h // bit * 2 + step) * bit + h % bit] for h in range(share)], axis=1
            )
            for j, bit in enumerate(bits)
        ],
        axis=0,
    )
    rows = x_ref[...].reshape(thirds * tok, x_ref.shape[2]).astype(F32)
    mid = rows + jnp.concatenate(
        [jnp.dot(attended, wo[k], preferred_element_type=F32) for k in range(blocks)], axis=1
    )
    normed = rms_scale(mid, gain[...]).astype(BF)
    arrive(1)
    hidden = []
    for k in range(blocks // 2):
        gate = jnp.dot(normed, wg[k], preferred_element_type=F32)
        up = jnp.dot(normed, wg[k + blocks // 2], preferred_element_type=F32)
        hidden.append((gate * jax.nn.sigmoid(gate) * up).astype(BF))
    hidden = jnp.concatenate(hidden, axis=1)
    arrive(2)
    final = mid + jnp.concatenate(
        [jnp.dot(hidden, wd[k], preferred_element_type=F32) for k in range(blocks)], axis=1
    )
    places = me * tok + lax.broadcasted_iota(jnp.int32, (tok, 1), 0)
    for j in range(thirds):
        length = lens[(req * 2 + step) * thirds + j]
        mine = final[j * tok : (j + 1) * tok]
        states[j] = jnp.where(places < length, mine, 0.0).astype(BF)


def cache_kernel(count, tok, info, perm, lens, one_ref, two_ref, *refs):
    w_refs, refs = refs[:count], refs[count:]
    bias, cos_ref, sin_ref, key_ref, value_ref, ws, sems = refs
    req, me = info[0], info[1]
    step = pl.program_id(0)
    size = 2 * pl.num_programs(0)
    rows = w_refs[0].shape[-2]
    model = key_ref.shape[-1]
    wide = ws.shape[2]
    used = [k for k in range(ws.shape[0]) if (k + 1) * wide > model]

    @pl.when(step == 0)
    def _():
        copies = [
            pltpu.make_async_copy(
                ref.at[info[4 + k]], ws.at[k, pl.ds(at, rows), :], sems.at[i * ws.shape[0] + k]
            )
            for i, (ref, at, _) in enumerate(sources(w_refs, me))
            for k in used
        ]
        for copy in copies:
            copy.start()
        for copy in copies:
            copy.wait()

    normed = jnp.concatenate([one_ref[0], two_ref[0]], axis=0)
    places = me * tok + lax.broadcasted_iota(jnp.int32, (tok, 1), 0)
    valid = [places < lens[perm[req * size + 2 * step + n]] for n in range(2)]
    cosine = jnp.concatenate([cos_ref[...]] * 2, axis=0)
    sine = jnp.concatenate([sin_ref[...]] * 2, axis=0)

    def store(ref, piece, low):
        for n in range(2):
            mine = piece[n * tok : (n + 1) * tok]
            ref[n, :, low : low + piece.shape[1]] = jnp.where(valid[n], mine, 0.0).astype(BF)

    for k in used:
        low, high = max(k * wide, model), (k + 1) * wide
        piece = jnp.dot(normed, ws[k, :, low - k * wide :], preferred_element_type=F32)
        piece = piece + bias[:, low:high]
        cut = min(max(2 * model, low), high)
        if low < cut:
            store(key_ref, turn(piece[:, : cut - low], cosine, sine), low - model)
        if cut < high:
            store(value_ref, piece[:, cut - low :], cut - 2 * model)


def local(
    prompts,
    perm,
    lengths,
    norm_attn,
    norm_mlp,
    qkv_train,
    qkv_bias,
    out_train,
    gateup_train,
    down_train,
):
    count, tok, width = prompts.shape
    groups = lax.axis_size("seq")
    parts = lax.axis_size("req")
    total = groups * tok
    me = lax.axis_index("seq").astype(jnp.int32)
    req = lax.axis_index("req").astype(jnp.int32)
    share = groups // 2
    heads = HEADS // share
    thirds = count // 2
    bits = [4, 2, 4] if groups == 8 else [share] * thirds
    halves = [lax.rem(lax.div(me, jnp.int32(bit)), jnp.int32(2)) for bit in bits]
    whiches = [lax.div(me, jnp.int32(2 * bit)) * bit + lax.rem(me, jnp.int32(bit)) for bit in bits]
    own_w = heads * HD
    anywhere = pl.BlockSpec(memory_space=pl.ANY)

    normed = rms_scale(prompts, norm_attn).astype(BF)

    cosine, sine = tables(total)
    chunk = 256
    blocks = qkv_train.shape[1] // chunk

    def attend(j, x_parts, weights):
        n_x, n_w = len(x_parts), len(weights)
        slot = req * count + halves[j] * thirds + j
        info = jnp.concatenate([jnp.stack([req, me, slot, whiches[j]]), relative])
        bias = lax.dynamic_index_in_dim(
            qkv_bias.reshape(3, share, own_w), whiches[j], 1, keepdims=False
        ).reshape(1, 3 * own_w)
        return pl.pallas_call(
            functools.partial(attend_kernel, j, n_x, n_w, tok, heads, chunk, blocks),
            out_shape=jax.ShapeDtypeStruct((total, own_w), BF),
            grid_spec=pltpu.PrefetchScalarGridSpec(
                num_scalar_prefetch=2,
                grid=(1,),
                in_specs=[anywhere] * (n_x + n_w)
                + [
                    pl.BlockSpec((1, 3 * own_w), lambda i, *_: (0, 0)),
                    pl.BlockSpec((total, 128), lambda i, *_: (0, 0)),
                    pl.BlockSpec((total, 128), lambda i, *_: (0, 0)),
                ],
                out_specs=pl.BlockSpec((total, own_w), lambda i, *_: (0, 0)),
                scratch_shapes=[
                    pltpu.VMEM((total, width), BF),
                    pltpu.VMEM((width, 3 * own_w), BF),
                    pltpu.VMEM((heads, total, HD), BF),
                    pltpu.VMEM((heads, total, HD), BF),
                    pltpu.VMEM((heads, total, 128), BF),
                    pltpu.SemaphoreType.DMA((groups + 6 * groups,)),
                ],
            ),
            compiler_params=pltpu.CompilerParams(vmem_limit_bytes=VMEM),
            cost_estimate=pl.CostEstimate(
                flops=1_000_000_000, bytes_accessed=1_000_000, transcendentals=0
            ),
            name="attend",
        )(info, lengths, *x_parts, *weights, bias, cosine, sine)

    def spread_heads(out):
        return lax.all_to_all(
            out.reshape(1, groups, tok, own_w), "seq", split_axis=1, concat_axis=1, tiled=True
        )

    rows_o = out_train.shape[0]
    qkv = qkv_train.astype(BF)
    gateup = gateup_train.astype(BF)
    tail = jnp.concatenate([out_train.astype(BF), down_train.astype(BF)], axis=0)
    if groups == 8:
        def prompt_of(j, other):
            side = 1 - halves[j] if other else halves[j]
            return lax.dynamic_index_in_dim(normed, side * thirds + j, 0, keepdims=False)

        def halved(array):
            rows = array.shape[1] // 2
            return [array[:, :rows], array[:, rows:]]

        def first_way(held):
            return [*held, swap(held[0], 2), swap(held[1], 4)]

        def second_way(held):
            upper, lower, upper_x, lower_y = held
            upper, lower = jnp.stack([upper, upper_x]), jnp.stack([lower, lower_y])
            return [upper, lower, swap(upper, 4), swap(lower, 2)]

        def both_cores(held):
            return [*held, *(swap(array, 1) for array in held)]

        kinds = [[j for j in range(thirds) if bits[j] == bit] for bit in (4, 2)]
        far = [jnp.stack([prompt_of(j, True) for j in kind]) for kind in kinds]
        near = [jnp.stack([prompt_of(j, False) for j in kind]) for kind in kinds]
        along_y = swap(jnp.concatenate([far[0], near[1]]), 4)
        along_x = swap(jnp.concatenate([far[1], near[0]]), 2)

        def round_trip(array):
            held = [array]
            for _ in range(parts - 1):
                held.append(hop(held[-1]))
            return held

        qkv_hops = round_trip(after(qkv, normed))
        gu_hops = round_trip(after(gateup, qkv_hops[1]))

        *qkv_hops, along_x, along_y, gu_hops[2], tail = gate(
            [*qkv_hops, along_x, along_y, gu_hops[2], tail]
        )
        qkv_c = jnp.stack(qkv_hops)
        gu_hops[3] = hop(gu_hops[2])
        n_y, n_x = len(kinds[0]), len(kinds[1])
        far_x = swap(along_y[:n_y], 2)
        far_y = swap(along_x[:n_x], 4)
        w_at = first_way(halved(qkv_c))
        tails = round_trip(after(tail, gu_hops[3]))
        gu_c = jnp.stack(gu_hops)

        far_x, far_y, *held = gate([far_x, far_y, *w_at, *tails])
        w_at, tails = held[:4], held[4:]
        w_at = second_way(w_at)
        to_caches = after(normed, tails[-1])
        pieces = [None] * thirds
        for i, j in enumerate(kinds[0]):
            pieces[j] = jnp.stack([near[0][i], along_x[n_x + i], along_y[i], far_x[i]])
        for i, j in enumerate(kinds[1]):
            pieces[j] = jnp.stack([near[1][i], along_x[i], along_y[n_y + i], far_y[i]])
        pieces = jnp.stack(pieces)
        x_parts = [pieces, swap(pieces, 1)]

        *w_at, x_parts[0], x_parts[1], gu_c = gate([*w_at, *x_parts, gu_c])
        qkv_w = both_cores(w_at)
        g_at = first_way(halved(gu_c))
        t_at = first_way(halved(jnp.stack(tails)))

        relative = steps_back()
        out = attend(0, x_parts, qkv_w)

        out, *held = gate([out, *t_at, *g_at])
        attended = [spread_heads(out)]

        t_at, g_at = second_way(held[:4]), held[4:]
        out = attend(1, [after(x_parts[0], out), x_parts[1]], qkv_w)

        out, attended[0], *held = gate([out, attended[0], *t_at, *g_at])
        attended.append(spread_heads(out))
        g_at, tail_w = second_way(held[4:]), both_cores(held[:4])
        out = attend(2, [after(x_parts[0], out), x_parts[1]], qkv_w)

        out, attended[1], *held = gate([out, attended[1], *g_at, *tail_w])
        attended.append(spread_heads(out))
        gu_w, tail_w = both_cores(held[:4]), held[4:]
    else:
        relative = jnp.arange(parts, dtype=jnp.int32)
        qkv_c, gu_c, tail_c = (lax.all_gather(w, "req", axis=0) for w in (qkv, gateup, tail))
        qkv_w, gu_w = whole(qkv_c), whole(gu_c)
        tail_w = whole(tail_c[:, :rows_o]) + whole(tail_c[:, rows_o:])
        everything = lax.all_gather(normed, "seq", axis=0)
        to_caches = normed
        if own_w == chunk:
            attend_w = qkv_w
        else:
            full = qkv_w[0][0].transpose(1, 0, 2).reshape(width, 3, share, own_w)
            attend_w = lax.dynamic_index_in_dim(full, whiches[0], 2, keepdims=False)
            attend_w = [attend_w.reshape(1, width, 3 * own_w)]
        outs = []
        for j in range(thirds):
            mine = lax.dynamic_index_in_dim(everything, halves[j] * thirds + j, 1, keepdims=False)
            outs.append(attend(j, [mine], attend_w))
        attended = [spread_heads(out) for out in outs]


    info = jnp.concatenate([jnp.stack([req, me, jnp.int32(0), jnp.int32(0)]), relative])
    n_w = len(gu_w)

    third = pl.BlockSpec((thirds, tok, width), lambda i, *_: (i, 0, 0))
    states = pl.pallas_call(
        functools.partial(mlp_kernel, n_w, tok, bits, [a.shape[0] for a in attended]),
        out_shape=jax.ShapeDtypeStruct((count, tok, width), BF),
        grid_spec=pltpu.PrefetchScalarGridSpec(
            num_scalar_prefetch=2,
            grid=(2,),
            in_specs=[third]
            + [anywhere] * (len(attended) + n_w + len(tail_w))
            + [pl.BlockSpec((1, width), lambda i, *_: (0, 0))],
            out_specs=third,
            scratch_shapes=[
                pltpu.VMEM((thirds, groups, tok, own_w), BF),
                pltpu.VMEM((parts, width, out_train.shape[1]), BF),
                pltpu.VMEM((parts, width, gateup_train.shape[1]), BF),
                pltpu.VMEM((parts, groups * down_train.shape[0], down_train.shape[1]), BF),
                pltpu.SemaphoreType.DMA((thirds + 6 * groups * parts,)),
            ],
        ),
        compiler_params=pltpu.CompilerParams(vmem_limit_bytes=VMEM),
        cost_estimate=pl.CostEstimate(
            flops=1_000_000_000, bytes_accessed=1_000_000, transcendentals=0
        ),
        name="feed_forward",
    )(info, lengths, prompts, *attended, *gu_w, *tail_w, norm_mlp.reshape(1, width))

    everyone = lax.all_gather(to_caches, "req", axis=0, tiled=True)
    own_rows = pl.BlockSpec((tok, 128), lambda i, info, *_: (info[1], 0))
    n_w = len(qkv_w)
    keys, values = pl.pallas_call(
        functools.partial(cache_kernel, n_w, tok),
        out_shape=[jax.ShapeDtypeStruct((count, tok, width), BF)] * 2,
        grid_spec=pltpu.PrefetchScalarGridSpec(
            num_scalar_prefetch=3,
            grid=(count // 2,),
            in_specs=[
                pl.BlockSpec(
                    (1, tok, width),
                    lambda i, info, perm, lens: (perm[info[0] * count + 2 * i], 0, 0),
                ),
                pl.BlockSpec(
                    (1, tok, width),
                    lambda i, info, perm, lens: (perm[info[0] * count + 2 * i + 1], 0, 0),
                ),
            ]
            + [anywhere] * n_w
            + [
                pl.BlockSpec((1, 3 * width), lambda i, *_: (0, 0)),
                own_rows,
                own_rows,
            ],
            out_specs=[pl.BlockSpec((2, tok, width), lambda i, *_: (i, 0, 0))] * 2,
            scratch_shapes=[
                pltpu.VMEM((parts, width, qkv_train.shape[1]), BF),
                pltpu.SemaphoreType.DMA((2 * groups * parts,)),
            ],
        ),
        compiler_params=pltpu.CompilerParams(vmem_limit_bytes=VMEM),
        cost_estimate=pl.CostEstimate(
            flops=1_000_000_000, bytes_accessed=1_000_000, transcendentals=0
        ),
        name="caches",
    )(after(info, states), perm, lengths, everyone, everyone, *qkv_w, qkv_bias.reshape(1, 3 * width), cosine, sine)
    return (states, keys, values)


def solution(mesh):
    placed = (
        P("req", "seq", None),
        P(),
        P(),
        P(),
        P(),
        P("seq", "req"),
        P(),
        P("seq", "req"),
        P("seq", "req"),
        P("seq", "req"),
    )
    return jax.shard_map(
        local,
        mesh=mesh,
        in_specs=placed,
        out_specs=(P("req", "seq", None), P("req", "seq", None), P("req", "seq", None)),
        check_vma=False,
    )
```
